512 devices in a mesh: role: 2 (over y_lo), ep: 128 (over z, x, core), tp: 2 (over y_hi).
Axes of the slice: x: 4, y: 4 (y_hi: 2, y_lo: 2; y = y_hi * 2 + y_lo), z: 16, core: 2. Of those that a mesh axis runs over, the one named last changes fastest.
Arguments:
- routes: int32 [4096, 8], P(('role', 'ep')), may hold values from 0 to 127, all different within a row; in each aligned block of 16 rows (0 to 15, 16 to 31, ...) at most 2 rows name the same one
- gate_weights: float32 [4096, 8], P(('role', 'ep')), may hold values from 0.05 to 0.5
- expert_hidden: bfloat16 [256, 256, 1024], P(('role', 'ep'), None, 'tp'), may hold values from -6 to 6
- down_weight: bfloat16 [128, 1024, 3584], P('ep', None, 'tp'), may hold values from -0.1875 to 0.1875
- queries: bfloat16 [256, 2, 2, 128, 576], P(('role', 'ep'), None, None, 'tp'), may hold values from -4 to 4
- new_latents: bfloat16 [256, 2, 2, 576], P(('role', 'ep')), may hold values from -4 to 4
- lengths: int32 [256], replicated, may hold values from 128 to 1024
- destinations: int32 [128], replicated, may hold values from 0 to 127, as said below
- latent_cache: bfloat16 [256, 1024, 576], P(('role', 'ep'), 'tp'), may hold values from -4 to 4
Outputs:
- moe_output: bfloat16 [4096, 3584], P(('role', 'ep'), 'tp')
- attention_output: bfloat16 [256, 2, 2, 128, 512], P(('role', 'ep'), None, None, 'tp')
The draws below stay inside these ranges and needn't reach their ends.
Inputs may be any that keep to these rules, and one draw needn't show every extreme that they name: `routes`: in each aligned block of 16 rows no expert is named more than 2 times. destinations[i] is i or i XOR 1, and destinations[destinations[i]] = i.
All inputs are finite; a program needn't handle non-finite values.
Results may differ from the reference program's by a relative error of at most 0.0049.
Values may be sent and summed in bfloat16 or wider, within the bound.
A program may use at most 64 MiB of HBM per device.

```python
import math
import jax
import jax.numpy as jnp
import numpy as np
from jax import lax

D = 3584
HID = 1024
HEADS = 128
LAT = 576
VLAT = 512
TOP = 8
TOK_DEV = 16
CTX = 1024
GROUPS = 2
STEPS = 2
SOURCES = 128
EXPERTS = 128
CAP = 2
TOKENS = 4096
REQS = 256
N_ROLE = 2


def draw_latent_cache(key, part):
    key = jax.random.fold_in(key, 1)
    values = jnp.clip(jax.random.normal(key, (REQS, CTX, LAT), jnp.float32), -4.0, 4.0)
    return values.astype(jnp.bfloat16)


def draw_queries(key, part):
    key = jax.random.fold_in(key, 2)
    values = jnp.clip(jax.random.normal(key, (REQS, GROUPS, STEPS, HEADS, LAT), jnp.float32), -4.0, 4.0)
    return values.astype(jnp.bfloat16)


def draw_destinations(key, part):
    key = jax.random.fold_in(key, 3)
    flips = jax.random.randint(key, (SOURCES // 2,), 0, 2).astype(jnp.int32)
    indices = jnp.arange(SOURCES, dtype=jnp.int32)
    return jnp.bitwise_xor(indices, jnp.repeat(flips, 2)).astype(jnp.int32)


def place_ends(result, stream_key, low, largest):
    place = [jax.random.randint(jax.random.fold_in(stream_key, axis), (), 0, length) for axis, length in enumerate(result.shape)]
    main_axis = result.shape.index(max(result.shape))
    next_to = place[:main_axis] + [(place[main_axis] + 1) % result.shape[main_axis]] + place[main_axis + 1:]
    return result.at[tuple(place)].set(low).at[tuple(next_to)].set(largest)


def block_levels(key, shape, pieces, low, top_value):
    def one(dim, shards_of):
        draws = jax.random.uniform(jax.random.fold_in(jax.random.fold_in(key, 6), dim), (shards_of,), jnp.float32, low / len(pieces), top_value / len(pieces))
        return jnp.repeat(jnp.exp(draws), shape[dim] // shards_of).reshape((-1,) + (1,) * (len(shape) - dim - 1))

    loudness = one(*pieces[0])
    for cut in pieces[1:]:
        loudness = loudness * one(*cut)
    return loudness


def routed_block(rng, own, number, rows, number_of, top, reach, skew):
    ranking = jax.random.permutation(rng, number_of)
    packed, ordinary = shares(number_of, rows * top, reach, skew, True), shares(number_of, rows * top, reach, skew, False)
    places = jnp.arange(number_of)

    def named(tallies, rotation):
        used = int((tallies > 0).sum())
        fixed = max(1, used // 4)
        passed = fixed + (places - fixed + rotation * (used - fixed)) % max(1, number_of - fixed)
        return jnp.zeros((number_of,), jnp.int32).at[ranking[jnp.where(places < fixed, places, passed)]].set(jnp.asarray(tallies, jnp.int32))

    tallies = jnp.where(number % 4 == 0, named(packed, number // 4), named(ordinary, number - number // 4 - 1))
    mixed = jax.random.permutation(jax.random.fold_in(own, 3), number_of)
    giver, taker = mixed[0:number_of // 2 * 2:2], mixed[1:number_of // 2 * 2:2]
    slack = jnp.minimum(tallies[giver] - 1, reach - tallies[taker]) // 2
    slack = jnp.where((giver == ranking[0]) | (taker == ranking[0]) | (tallies[taker] == 0), 0, jnp.maximum(slack, 0))
    passed = jax.random.randint(jax.random.fold_in(own, 4), (number_of // 2,), 0, 1 << 20) % (slack + 1)
    tallies = tallies.at[giver].add(-passed).at[taker].add(passed)
    items = jnp.searchsorted(jnp.cumsum(tallies), jnp.arange(rows * top), side="right").astype(jnp.int32)
    grid = items.reshape(top, rows).T
    grid = grid[jax.random.permutation(jax.random.fold_in(own, 1), rows)]
    rotation = jax.random.randint(jax.random.fold_in(own, 2), (rows, 1), 0, top)
    return jnp.take_along_axis(grid, (jnp.arange(top)[None, :] + rotation) % top, axis=1)


def shares(amount, total, reach, slope, full):
    weights = [(1 << 20) // math.isqrt(standing ** slope) + 1 for standing in range(1, amount + 1)]
    largest = reach if full else min(reach, max(-(-total // amount), total * weights[0] // sum(weights)))
    least = 1 if total - largest >= amount - 1 else 0
    counts, rest = [largest] + [least] * (amount - 1), total - largest - least * (amount - 1)
    while rest > 0:
        free = [i for i in range(1, amount) if counts[i] < largest] or [i for i in range(1, amount) if counts[i] < reach]
        mass, remaining = sum([weights[i] for i in free]), rest
        for i in free:
            extra = min(reach - counts[i], max(1, remaining * weights[i] // mass), rest)
            counts[i] = counts[i] + extra
            rest = rest - extra
    return np.array(counts)


def centred(stream_key, extent, spread, reach, shards=(), kind=jnp.bfloat16):
    array = jax.random.normal(stream_key, extent, jnp.float32) * spread
    if len(shards) > 0:
        array = block_levels(stream_key, extent, shards, -0.22, 0.18) * array
    return jnp.clip(array, min=-reach, max=reach).astype(kind)


def setup_inputs(seed: int = 0) -> dict:
    arg_keys = jax.random.split(jax.random.key(seed), 10)
    routes_keys = jax.random.split(jax.random.fold_in(arg_keys[0], 1), TOKENS // TOK_DEV)
    routes_turns = jax.random.permutation(jax.random.fold_in(arg_keys[0], 3), TOKENS // TOK_DEV)
    routes = jax.vmap(lambda own, number: routed_block(jax.random.fold_in(arg_keys[0], 2), own, number, TOK_DEV, EXPERTS, TOP, CAP, 2))(routes_keys, routes_turns).reshape((TOKENS, TOP))
    gate_weights = jnp.clip(jnp.exp(math.log(0.5) - 2.3025851 * jax.random.uniform(arg_keys[1], (TOKENS, TOP), jnp.float32) ** block_levels(arg_keys[1], (TOKENS, TOP), ((0, 256),), -0.2, 0.2)), 0.05, 0.5)
    expert_hidden = centred(arg_keys[2], (N_ROLE * EXPERTS, SOURCES * CAP, HID), 1.0, 6.0, ((0, 256), (2, 2)))
    down_weight = centred(arg_keys[3], (EXPERTS, HID, D), HID ** -0.5, 0.1875, ((0, 128), (2, 2)))
    queries = draw_queries(jax.random.fold_in(arg_keys[9], 71), 0)
    new_latents = centred(arg_keys[5], (REQS, GROUPS, STEPS, LAT), 1.0, 4.0, ((0, 256),))
    lengths = place_ends(jax.random.randint(arg_keys[6], (REQS,), CTX // 8, CTX + 1), jax.random.fold_in(arg_keys[6], 1), CTX // 8, CTX).astype(jnp.int32)
    destinations = draw_destinations(jax.random.fold_in(arg_keys[9], 71), 0)
    latent_cache = draw_latent_cache(jax.random.fold_in(arg_keys[9], 71), 0)
    return dict(routes=routes, gate_weights=gate_weights, expert_hidden=expert_hidden, down_weight=down_weight, queries=queries, new_latents=new_latents, lengths=lengths, destinations=destinations, latent_cache=latent_cache)


SCORE_SCALE = 0.07216878364870322
VERY_LOW = -1.0e30


def slot_numbers(pick_table):
    flat_picks = pick_table.reshape(-1)
    pick_count = flat_picks.shape[0]
    same_pick = (flat_picks[:, None] == flat_picks[None, :]).astype(jnp.int32)
    earlier = (lax.broadcasted_iota(jnp.int32, (pick_count, pick_count), 1) < lax.broadcasted_iota(jnp.int32, (pick_count, pick_count), 0)).astype(jnp.int32)
    return jnp.sum(same_pick * earlier, axis=1).astype(jnp.int32).reshape(pick_table.shape)


def project(operands):
    hidden, weight = operands
    return jnp.einsum("brh,hd->brd", hidden.astype(jnp.float32), weight.astype(jnp.float32), precision=lax.Precision.HIGHEST).astype(jnp.bfloat16)


def reference(routes, gate_weights, expert_hidden, down_weight, queries, new_latents, lengths, destinations, latent_cache):
    blocks = routes.reshape(N_ROLE * SOURCES, TOK_DEV * TOP)
    slot_table = jax.vmap(slot_numbers)(blocks).reshape(TOKENS, TOP)
    rows_each = SOURCES * CAP
    by_expert = jnp.transpose(expert_hidden.reshape(N_ROLE, EXPERTS, rows_each, HID), (1, 0, 2, 3))
    outputs = lax.map(project, (by_expert, down_weight))
    flat_rows = outputs.reshape(EXPERTS * N_ROLE * rows_each, D)
    token_ids = jnp.arange(TOKENS, dtype=jnp.int32)
    section = token_ids // (SOURCES * TOK_DEV)
    source_ids = (token_ids // TOK_DEV) % SOURCES
    summed = jnp.zeros((TOKENS, D), jnp.float32)
    for pick_num in range(TOP):
        row_index = routes[:, pick_num] * (N_ROLE * rows_each) + section * rows_each + source_ids * CAP + slot_table[:, pick_num]
        summed = summed + gate_weights[:, pick_num:pick_num + 1].astype(jnp.float32) * flat_rows[row_index].astype(jnp.float32)
    moe_output = summed.astype(jnp.bfloat16)

    span_len = GROUPS * STEPS

    def attend_row(row_id):
        decoding = row_id >= SOURCES
        handed = destinations[row_id % SOURCES].astype(jnp.int32)
        second = jnp.where(decoding, handed, row_id).astype(jnp.int32)
        results = []
        for group_num in range(GROUPS):
            if group_num == 0:
                source = row_id
                visible_count = jnp.zeros((), jnp.int32)
            else:
                source = second
                visible_count = jnp.where(decoding, span_len, STEPS).astype(jnp.int32)
            cached = latent_cache[source]
            prior_keys = new_latents[source].reshape(span_len, LAT)
            own_keys = new_latents[row_id, group_num]
            all_keys = jnp.concatenate([cached, prior_keys, own_keys], axis=0).astype(jnp.float32)
            query_rows = queries[row_id, group_num].astype(jnp.float32)
            scores = jnp.einsum("shl,pl->shp", query_rows, all_keys, precision=lax.Precision.HIGHEST) * SCORE_SCALE
            positions = jnp.arange(CTX + span_len + STEPS, dtype=jnp.int32)[None, :]
            step_ids = jnp.arange(STEPS, dtype=jnp.int32)[:, None]
            cached_ok = positions < lengths[source]
            prior_ok = (positions - CTX) < visible_count
            own_ok = (positions - CTX - span_len) <= step_ids
            allowed = jnp.where(positions < CTX, cached_ok, jnp.where(positions < CTX + span_len, prior_ok, own_ok))
            kept_scores = jnp.where(allowed[:, None, :], scores, VERY_LOW)
            row_top = jnp.max(kept_scores, axis=-1, keepdims=True)
            weights = jnp.where(allowed[:, None, :], jnp.exp(kept_scores - row_top), 0.0)
            weights = weights / jnp.sum(weights, axis=-1, keepdims=True)
            results.append(jnp.einsum("shp,pv->shv", weights, all_keys[:, :VLAT], precision=lax.Precision.HIGHEST).astype(jnp.bfloat16))
        return jnp.stack(results)

    attention_output = lax.map(attend_row, jnp.arange(REQS, dtype=jnp.int32))
    return moe_output, attention_output
```

```python
import functools
import types

import jax
import jax.numpy as jnp
from jax import lax
from jax.experimental import pallas as pl
from jax.experimental.pallas import tpu as pltpu
from jax.sharding import PartitionSpec as P

MESH = pl.DeviceIdType.MESH
F32 = jnp.float32
BF16 = jnp.bfloat16

SCORE_SCALE = 0.07216878364870322
VERY_LOW = -1e30
VLAT = 512
LAT = 576
SHARD = 512
PLANES = 16
LOW = 8
TOK = 16
WIDTH = 1792
HALF = 512
QROWS = 128
SPAN = 16
CHUNKS = (896, 896)

OFFSETS = (1, -3, 5, -7, 3, -1, 7, -5, -4, 4, 8, 2, -2, 6, -6, 0)
SENT = 11
FIRST_HOPS = ((0, 4, 1), (4, 4, -1), (8, 1, 2), (9, 2, -2))
SECOND_HOPS = (-2, 2, -6, 6)


def remote(src, dst, send, recv, device):
    return pltpu.make_async_remote_copy(
        src_ref=src, dst_ref=dst, send_sem=send, recv_sem=recv, device_id=device, device_id_type=MESH
    )


def wait_for(ref, sem):
    pltpu.make_async_copy(ref, ref, sem).wait()


def iota(shape, dim):
    return lax.broadcasted_iota(jnp.int32, shape, dim)


def dot(a, b, b_dim=0):
    return lax.dot_general(a, b, (((1,), (b_dim,)), ((), ())), preferred_element_type=F32)


def split(value):
    high = value.astype(BF16)
    return high, (value - high.astype(F32)).astype(BF16)


def offset_of(block):
    value = jnp.zeros_like(block)
    for number, offset in enumerate(OFFSETS):
        value = jnp.where(block == number, offset, value)
    return value


def signed_gates(routes, gates):
    names = iota((TOK, 128), 1)
    picked = jnp.zeros((TOK, 128), F32)
    weight = jnp.zeros((TOK, 128), F32)
    for pick in range(routes.shape[1]):
        here = routes[:, pick : pick + 1] == names
        picked = jnp.where(here, 1.0, picked)
        weight = jnp.where(here, gates[:, pick : pick + 1], weight)
    earlier = jnp.where(iota((TOK, TOK), 1) < iota((TOK, TOK), 0), 1.0, 0.0).astype(BF16)
    slot = dot(earlier, picked.astype(BF16))
    return jnp.where(slot > 0.5, -weight, weight)


def scores_of(query, keys, span, length, tp, extra_ok):
    visible = []
    scores = []
    for number, key in enumerate(keys):
        first = (tp if number == 0 else 1 - tp) * SHARD
        ok = iota((1, SHARD), 1) + first < length
        visible.append(ok)
        scores.append(jnp.where(ok, dot(query, key[...]) * SCORE_SCALE, VERY_LOW))
    scores.append(jnp.where(extra_ok, dot(query, span[...], 1) * SCORE_SCALE, VERY_LOW))
    visible.append(extra_ok)
    top = functools.reduce(jnp.maximum, [jnp.max(s, axis=1, keepdims=True) for s in scores])
    parts = [jnp.where(ok, jnp.exp(s - top), 0.0) for s, ok in zip(scores, visible)]
    total = sum(jnp.sum(part, axis=1, keepdims=True) for part in parts)
    value = dot(parts[-1].astype(BF16), span[:, :VLAT])
    for part, key in zip(parts, keys):
        value = value + dot(part.astype(BF16), key[:VLAT, :], 1)
    return top, total, value


def kernel(
    routes_hbm,
    gates_hbm,
    hidden_hbm,
    down_hbm,
    queries_hbm,
    span_hbm,
    lengths_hbm,
    destinations_hbm,
    cache_hbm,
    moe_ref,
    attention_ref,
    *scratch,
):
    ref = named(scratch)
    count = len(CHUNKS)
    starts = [sum(CHUNKS[:c]) for c in range(count)]

    role, ep, tp = lax.axis_index("role"), lax.axis_index("ep"), lax.axis_index("tp")
    z, low = ep // LOW, ep % LOW

    def along_z(step):
        return {"ep": lax.rem(z + step + PLANES, PLANES) * LOW + low}

    def in_plane(step):
        return {"ep": z * LOW + lax.rem(low + step, LOW)}

    partner = {"tp": 1 - tp}
    other_role = {"role": 1 - role}
    sibling = {"ep": z * LOW + low + 1 - 2 * (low % 2)}

    barrier = pltpu.get_barrier_semaphore()

    def greet(device):
        pl.semaphore_signal(barrier, inc=1, device_id=device, device_id_type=MESH)

    greet(partner)
    greet(other_role)

    @pl.loop(1, LOW)
    def _(step):
        greet(in_plane(step))

    @pl.loop(1, PLANES)
    def _(step):
        greet(along_z(step))

    local = ref.local_sem

    def fetch(number, source, target):
        copy = pltpu.make_async_copy(source, target, local.at[number])
        copy.start()
        return copy

    routes_here = fetch(0, routes_hbm, ref.routes)
    gates_here = fetch(1, gates_hbm, ref.gates)
    hidden_here = fetch(2, hidden_hbm, ref.hidden)
    down_here = fetch(3, down_hbm, ref.down)
    cache_here = fetch(4, cache_hbm, ref.cache)
    queries_here = fetch(5, queries_hbm, ref.queries)
    span_here = fetch(6, span_hbm, ref.span)
    lengths_here = fetch(7, lengths_hbm, ref.lengths)
    destinations_here = fetch(8, destinations_hbm, ref.destinations)

    pl.semaphore_wait(barrier, 2 + LOW - 1 + PLANES - 1)

    hidden_copy = remote(hidden_hbm, ref.hidden_in, ref.tp_sem.at[0], ref.tp_sem.at[1], partner)
    hidden_copy.start()
    swap_copy = remote(
        queries_hbm.at[pl.ds(QROWS, QROWS)], ref.query_swap, ref.swap_sem.at[0], ref.swap_sem.at[1], sibling
    )

    @pl.when(role == 1)
    def _():
        swap_copy.start()

    routes_here.wait()
    gates_here.wait()
    own_gates = signed_gates(ref.routes[...], ref.gates[...])
    ref.gates_out[...] = own_gates
    for number, offset in enumerate(OFFSETS):
        rows = pl.ds(number * TOK, TOK)
        if offset == 0:
            ref.gates_in[rows, :] = own_gates
        else:
            remote(
                ref.gates_out, ref.gates_in.at[rows], ref.gate_sem.at[0], ref.gate_sem.at[1], along_z(offset)
            ).start()

    index = iota((256, 1), 0)
    block = (index >> 1) & 15
    raw = (((z - offset_of(block)) & 15) << 4) + (((low + (index >> 5)) & 7) << 1) + (index & 1)
    order = jnp.where(iota((256, 256), 1) == raw, 1.0, 0.0).astype(BF16)
    ref.order[...] = order
    hidden_here.wait()
    ref.hidden_own[...] = dot(order, ref.hidden[...]).astype(BF16)
    down_here.wait()
    own_units = pl.ds(pl.multiple_of(tp * HALF, HALF), HALF)
    other_units = pl.ds(pl.multiple_of((1 - tp) * HALF, HALF), HALF)
    for c in range(count):
        columns = slice(starts[c], starts[c] + CHUNKS[c])
        ref.first_half[:, columns] = dot(ref.hidden_own[...], ref.down[own_units, columns])

    hidden_copy.wait_recv()
    ref.hidden_own[...] = dot(ref.order[...], ref.hidden_in[...]).astype(BF16)
    x_sem = ref.x_sem
    for c in range(count):
        columns = slice(starts[c], starts[c] + CHUNKS[c])
        rows_out = ref.first_half[:, columns] + dot(ref.hidden_own[...], ref.down[other_units, columns])
        rows_out = rows_out.astype(BF16)
        ref.x_in[c][0:32, :] = rows_out[0:32]
        ref.x_out[c][...] = rows_out[32:]

        @pl.loop(1, LOW)
        def _(step, c=c):
            rows = pl.ds(pl.multiple_of(step * 32 - 32, 32), 32)
            rows_in = pl.ds(pl.multiple_of(step * 32, 32), 32)
            remote(
                ref.x_out[c].at[rows], ref.x_in[c].at[rows_in], x_sem.at[0, c], x_sem.at[1, c], in_plane(step)
            ).start()

    cache_here.wait()
    cache_copy = remote(ref.cache, ref.cache_in, ref.tp_sem.at[2], ref.tp_sem.at[3], partner)
    cache_copy.start()
    queries_here.wait()
    span_here.wait()
    lengths_here.wait()
    destinations_here.wait()
    length = ref.lengths[role * 128 + ep]
    flipped = jnp.broadcast_to(ref.destinations[ep], (QROWS, 1)) != ep
    ask_copy = remote(ref.query_out, ref.query_in, ref.role_sem.at[0], ref.role_sem.at[1], other_role)

    @pl.when(role == 1)
    def _():
        swap_copy.wait_recv()
        swapped = ref.query_swap[...].astype(F32)
        ref.query_out[...] = jnp.where(flipped, swapped, ref.queries[QROWS:, :].astype(F32)).astype(BF16)
        ask_copy.start()

    wait_for(ref.gates_in.at[pl.ds(0, 15 * TOK)], ref.gate_sem.at[1])
    gates_in = ref.gates_in[...]
    column = iota((128, 256), 1)
    expert = z * LOW + ((low - (column >> 5)) & 7)
    mine = iota((128, 256), 0) == expert
    pick_first = jnp.where(mine & ((column & 1) == 0), 1.0, 0.0).astype(BF16)
    pick_second = jnp.where(mine & ((column & 1) == 1), 1.0, 0.0).astype(BF16)
    first_high, first_low = split(jnp.maximum(gates_in, 0.0))
    second_high, second_low = split(jnp.maximum(-gates_in, 0.0))
    same_block = ((iota((256, 256), 1) >> 1) & 15) == (iota((256, 256), 0) >> 4)
    gates_high = jnp.where(same_block, dot(first_high, pick_first) + dot(second_high, pick_second), 0.0)
    gates_low = jnp.where(same_block, dot(first_low, pick_first) + dot(second_low, pick_second), 0.0)
    ref.gates_high[...] = gates_high.astype(BF16)
    ref.gates_low[...] = gates_low.astype(BF16)

    def combine(c):
        wait_for(ref.x_in[c].at[pl.ds(32, 224)], x_sem.at[1, c])
        rows_in = ref.x_in[c][...]
        sums = dot(ref.gates_high[...], rows_in) + dot(ref.gates_low[...], rows_in)
        ref.first_out[c][...] = sums[: SENT * TOK].astype(BF16)
        ref.kept[c][...] = sums[SENT * TOK :]
        for first, blocks, step in FIRST_HOPS:
            rows = pl.ds(first * TOK, blocks * TOK)
            remote(
                ref.first_out[c].at[rows], ref.first_in[c].at[rows], x_sem.at[2, c], x_sem.at[3, c], along_z(step)
            ).start()

    def collect(c):
        wait_for(ref.first_in[c], x_sem.at[3, c])
        got = ref.first_in[c][...].astype(F32)
        sums = ref.kept[c][0:64, :] + got[0:64] + got[64:128]
        ref.second_out[c][0:16, :] = (sums[0:16] + got[144:160]).astype(BF16)
        ref.second_out[c][16:32, :] = (sums[16:32] + got[128:144]).astype(BF16)
        ref.second_out[c][32:48, :] = (sums[32:48] + got[160:176]).astype(BF16)
        ref.second_out[c][48:64, :] = sums[48:64].astype(BF16)
        for number, step in enumerate(SECOND_HOPS):
            rows = pl.ds(number * TOK, TOK)
            remote(
                ref.second_out[c].at[rows], ref.second_in[c].at[rows], x_sem.at[4, c], x_sem.at[5, c], along_z(step)
            ).start()

    def finish(c):
        wait_for(ref.second_in[c], x_sem.at[5, c])
        got = ref.second_in[c][...].astype(F32)
        total = ref.kept[c][64:80, :] + (got[0:16] + got[16:32]) + (got[32:48] + got[48:64])
        moe_ref[:, starts[c] : starts[c] + CHUNKS[c]] = total.astype(BF16)

    keys = (ref.cache, ref.cache_in)
    step_of = iota((QROWS, SPAN), 0) >> 6
    key_of = iota((QROWS, SPAN), 1)
    answer_copy = remote(ref.answer_out, ref.answer_in, ref.role_sem.at[2], ref.role_sem.at[3], other_role)
    back_copy = remote(ref.answer_in, ref.answer_swap, ref.swap_sem.at[2], ref.swap_sem.at[3], sibling)

    def attend_first():
        cache_copy.wait_recv()

        @pl.when(role == 0)
        def _():
            ask_copy.wait_recv()
            top, total, value = scores_of(ref.query_in[...], keys, ref.span, length, tp, key_of < 4)
            ref.answer_out[:, :VLAT] = value.astype(BF16)
            lane = iota((QROWS, 128), 1)
            packed = jnp.zeros((QROWS, 128), F32)
            for number, figure in enumerate((top, total)):
                rest = figure
                for piece in range(3):
                    part = rest.astype(BF16).astype(F32)
                    rest = rest - part
                    packed = jnp.where(lane == number * 3 + piece, part, packed)
            ref.answer_out[:, VLAT:] = packed.astype(BF16)
            answer_copy.start()

    def attend_own():
        _, total, value = scores_of(ref.queries[:QROWS, :], keys, ref.span, length, tp, key_of <= step_of)
        attention_ref[:QROWS, :] = (value / total).astype(BF16)

        @pl.when(role == 0)
        def _():
            _, total, value = scores_of(ref.queries[QROWS:, :], keys, ref.span, length, tp, key_of <= step_of + 2)
            attention_ref[QROWS:, :] = (value / total).astype(BF16)

    def attend_back():
        @pl.when(role == 1)
        def _():
            answer_copy.wait_recv()
            back_copy.start()

    def attend_last():
        @pl.when(role == 1)
        def _():
            own_ok = (key_of >= 2) & (key_of <= step_of + 2)
            top, total, value = scores_of(ref.queries[QROWS:, :], (), ref.span, length, tp, own_ok)
            back_copy.wait_recv()
            answer = jnp.where(flipped, ref.answer_swap[...].astype(F32), ref.answer_in[...].astype(F32))
            figures = answer[:, VLAT:]
            far_top = figures[:, 0:1] + figures[:, 1:2] + figures[:, 2:3]
            far_total = figures[:, 3:4] + figures[:, 4:5] + figures[:, 5:6]
            best = jnp.maximum(top, far_top)
            near, far = jnp.exp(top - best), jnp.exp(far_top - best)
            value = near * value + far * answer[:, :VLAT]
            attention_ref[QROWS:, :] = (value / (near * total + far * far_total)).astype(BF16)

    combine(0)
    combine(1)
    attend_first()
    collect(0)
    attend_own()
    collect(1)
    attend_back()
    finish(0)
    attend_last()
    finish(1)

    hidden_copy.wait_send()
    cache_copy.wait_send()
    wait_for(ref.gates_in.at[pl.ds(0, 15 * TOK)], ref.gate_sem.at[0])
    for c in range(count):
        wait_for(ref.x_out[c], x_sem.at[0, c])
        wait_for(ref.first_out[c], x_sem.at[2, c])
        wait_for(ref.second_out[c], x_sem.at[4, c])

    @pl.when(role == 0)
    def _():
        answer_copy.wait_send()

    @pl.when(role == 1)
    def _():
        swap_copy.wait_send()
        ask_copy.wait_send()
        back_copy.wait_send()


def scratch_table():
    dma = pltpu.SemaphoreType.DMA

    def each(rows, kind=BF16):
        return [pltpu.VMEM((rows, width), kind) for width in CHUNKS]

    return dict(
        routes=pltpu.VMEM((TOK, 8), jnp.int32),
        gates=pltpu.VMEM((TOK, 8), F32),
        hidden=pltpu.VMEM((256, HALF), BF16),
        hidden_in=pltpu.VMEM((256, HALF), BF16),
        hidden_own=pltpu.VMEM((256, HALF), BF16),
        order=pltpu.VMEM((256, 256), BF16),
        down=pltpu.VMEM((2 * HALF, WIDTH), BF16),
        first_half=pltpu.VMEM((256, WIDTH), F32),
        cache=pltpu.VMEM((LAT, SHARD), BF16),
        cache_in=pltpu.VMEM((LAT, SHARD), BF16),
        queries=pltpu.VMEM((2 * QROWS, LAT), BF16),
        query_swap=pltpu.VMEM((QROWS, LAT), BF16),
        query_out=pltpu.VMEM((QROWS, LAT), BF16),
        query_in=pltpu.VMEM((QROWS, LAT), BF16),
        answer_out=pltpu.VMEM((QROWS, VLAT + 128), BF16),
        answer_in=pltpu.VMEM((QROWS, VLAT + 128), BF16),
        answer_swap=pltpu.VMEM((QROWS, VLAT + 128), BF16),
        span=pltpu.VMEM((SPAN, LAT), BF16),
        lengths=pltpu.SMEM((256,), jnp.int32),
        destinations=pltpu.SMEM((128,), jnp.int32),
        gates_out=pltpu.VMEM((TOK, 128), F32),
        gates_in=pltpu.VMEM((PLANES * TOK, 128), F32),
        gates_high=pltpu.VMEM((256, 256), BF16),
        gates_low=pltpu.VMEM((256, 256), BF16),
        x_out=each(224),
        x_in=each(256),
        first_out=each(SENT * TOK),
        first_in=each(SENT * TOK),
        kept=each(80, F32),
        second_out=each(64),
        second_in=each(64),
        local_sem=dma((9,)),
        tp_sem=dma((4,)),
        role_sem=dma((4,)),
        swap_sem=dma((4,)),
        gate_sem=dma((2,)),
        x_sem=dma((6, len(CHUNKS))),
    )


def named(refs):
    table = scratch_table()
    refs = jax.tree.unflatten(jax.tree.structure(table), refs)
    return types.SimpleNamespace(**refs)


def local(
    routes,
    gate_weights,
    expert_hidden,
    down_weight,
    queries,
    new_latents,
    lengths,
    destinations,
    latent_cache,
):
    span = jnp.pad(new_latents.reshape(4, LAT), ((0, SPAN - 4), (0, 0)))
    moe, attention = pl.pallas_call(
        kernel,
        out_shape=(
            jax.ShapeDtypeStruct((TOK, WIDTH), BF16),
            jax.ShapeDtypeStruct((2 * QROWS, VLAT), BF16),
        ),
        in_specs=[pl.BlockSpec(memory_space=pl.ANY)] * 9,
        out_specs=(pl.BlockSpec(memory_space=pltpu.VMEM),) * 2,
        scratch_shapes=jax.tree.leaves(scratch_table()),
        compiler_params=pltpu.CompilerParams(collective_id=0, has_side_effects=True, vmem_limit_bytes=40 * 2**20),
    )(
        routes,
        gate_weights,
        expert_hidden[0],
        down_weight[0],
        queries.reshape(2 * QROWS, LAT),
        span,
        lengths,
        destinations,
        jnp.swapaxes(latent_cache[0], 0, 1),
    )
    return moe, attention.reshape(1, 2, 2, QROWS // 2, VLAT)


def solution(mesh):
    placed = (
        P(("role", "ep"), None),
        P(("role", "ep"), None),
        P(("role", "ep"), None, "tp"),
        P("ep", None, "tp"),
        P(("role", "ep"), None, None, "tp", None),
        P(("role", "ep"), None, None, None),
        P(),
        P(),
        P(("role", "ep"), "tp", None),
    )
    return jax.shard_map(
        local,
        mesh=mesh,
        in_specs=placed,
        out_specs=(P(("role", "ep"), "tp"), P(("role", "ep"), None, None, "tp", None)),
        check_vma=False,
    )
```

```python
import functools
import types

import jax
import jax.numpy as jnp
from jax import lax
from jax.experimental import pallas as pl
from jax.experimental.pallas import tpu as pltpu
from jax.sharding import PartitionSpec as P

MESH = pl.DeviceIdType.MESH
F32 = jnp.float32
BF16 = jnp.bfloat16

SCORE_SCALE = 0.07216878364870322
VERY_LOW = -1e30
VLAT = 512
LAT = 576
SHARD = 512
PLANES = 16
LOW = 8
TOK = 16
WIDTH = 1792
HALF = 512
QROWS = 128
SPAN = 16
PART = 128
EDGE = 896

FAR = (5, -7, 7, -5, 8, 6, -6, 0)
NEAR = (1, -3, 3, -1, 4, -4, 2, -2)
HALVES = (FAR, NEAR)


class Chunk:
    def __init__(self, half, column, columns, sent, first_hops, planes, teams, second_hops):
        self.half = half
        self.columns = pl.ds(column, columns)
        self.sent = sent
        self.first_hops = first_hops
        self.planes = planes
        self.teams = teams
        self.second_hops = second_hops


CHUNKS = (
    Chunk(0, 0, EDGE, 5, ((0, 2, 1), (2, 2, -1), (4, 1, -2)), (-1, -1, 1, 1, 2, 0, 0, 0), (0, 1, 0, 1, 0, 0, 1, 2), (-6, 6)),
    Chunk(0, EDGE, EDGE, 5, ((0, 2, 1), (2, 2, -1), (4, 1, 2)), (-1, -1, 1, 1, -2, 0, 0, 0), (0, 1, 0, 1, 1, 0, 1, 2), (-6, 6)),
    Chunk(
        1, 0, WIDTH, 6, ((0, 2, 1), (2, 2, -1), (4, 1, -2), (5, 1, 2)), (-1, -1, 1, 1, 2, -2, 0, 0), (0, 1, 0, 1, 0, 1, 0, 1), (-2, 2)
    ),
)


def remote(src, dst, send, recv, device):
    return pltpu.make_async_remote_copy(
        src_ref=src, dst_ref=dst, send_sem=send, recv_sem=recv, device_id=device, device_id_type=MESH
    )


def wait_for(ref, sem):
    pltpu.make_async_copy(ref, ref, sem).wait()


def iota(shape, dim):
    return lax.broadcasted_iota(jnp.int32, shape, dim)


def dot(a, b, b_dim=0):
    return lax.dot_general(a, b, (((1,), (b_dim,)), ((), ())), preferred_element_type=F32)


def split(value):
    high = value.astype(BF16)
    return high, (value - high.astype(F32)).astype(BF16)


def choose(index, values):
    result = jnp.zeros_like(index)
    for number, value in enumerate(values):
        result = jnp.where(index == number, value, result)
    return result


def signed_gates(routes, gates, spread):
    names = iota((128, TOK), 0)
    picked = jnp.zeros((128, TOK), F32)
    weight = jnp.zeros((128, TOK), F32)
    for pick in range(routes.shape[0]):
        here = routes[pick : pick + 1, :] == names
        picked = jnp.where(here, 1.0, picked)
        weight = jnp.where(here, gates[pick : pick + 1, :], weight)
    earlier = jnp.where(iota((TOK, TOK), 0) < iota((TOK, TOK), 1), 1.0, 0.0).astype(BF16)
    slot = dot(picked.astype(BF16), earlier)
    spread[...] = jnp.zeros_like(spread)
    spread[:, :TOK] = jnp.where(slot > 0.5, -weight, weight)
    return spread[...].T[:TOK, :]


def scores_of(query, keys, span, length, tp, extra_ok):
    visible = []
    scores = []
    for number, key in enumerate(keys):
        first = (tp if number == 0 else 1 - tp) * SHARD
        ok = iota((1, SHARD), 1) + first < length
        visible.append(ok)
        scores.append(jnp.where(ok, dot(query, key[...]) * SCORE_SCALE, VERY_LOW))
    scores.append(jnp.where(extra_ok, dot(query, span[...], 1) * SCORE_SCALE, VERY_LOW))
    visible.append(extra_ok)
    top = functools.reduce(jnp.maximum, [jnp.max(s, axis=1, keepdims=True) for s in scores])
    parts = [jnp.where(ok, jnp.exp(s - top), 0.0) for s, ok in zip(scores, visible)]
    total = sum(jnp.sum(part, axis=1, keepdims=True) for part in parts)
    value = dot(parts[-1].astype(BF16), span[:, :VLAT])
    for part, key in zip(parts, keys):
        value = value + dot(part.astype(BF16), key[:VLAT, :], 1)
    return top, total, value


def kernel(
    routes_hbm,
    gates_hbm,
    hidden_hbm,
    down_hbm,
    queries_hbm,
    span_hbm,
    lengths_hbm,
    destinations_hbm,
    cache_hbm,
    moe_ref,
    attention_ref,
    *scratch,
):
    ref = named(scratch)

    role, ep, tp = lax.axis_index("role"), lax.axis_index("ep"), lax.axis_index("tp")
    z, low = ep // LOW, ep % LOW

    def along_z(step):
        return {"ep": lax.rem(z + step + PLANES, PLANES) * LOW + low}

    def in_plane(step):
        return {"ep": z * LOW + lax.rem(low + step, LOW)}

    partner = {"tp": 1 - tp}
    other_role = {"role": 1 - role}
    sibling = {"ep": z * LOW + low + 1 - 2 * (low % 2)}

    barrier = pltpu.get_barrier_semaphore()

    def greet(device):
        pl.semaphore_signal(barrier, inc=1, device_id=device, device_id_type=MESH)

    greet(partner)
    greet(other_role)

    @pl.loop(1, LOW)
    def _(step):
        greet(in_plane(step))

    for step in (1, -1, 2, -2):
        greet(along_z(step))

    local = ref.local_sem

    def fetch(number, source, target):
        copy = pltpu.make_async_copy(source, target, local.at[number])
        copy.start()
        return copy

    routes_here = fetch(0, routes_hbm, ref.routes)
    gates_here = fetch(1, gates_hbm, ref.gates)
    down_here = fetch(3, down_hbm, ref.down)
    cache_here = fetch(4, cache_hbm, ref.cache)
    queries_here = fetch(5, queries_hbm, ref.queries)
    span_here = fetch(6, span_hbm, ref.latents)
    lengths_here = fetch(7, lengths_hbm, ref.lengths)
    destinations_here = fetch(8, destinations_hbm, ref.destinations)

    def plane_rows(offset):
        return pl.ds(pl.multiple_of(((z - offset) & 15) * TOK, TOK), TOK)

    for half, offsets in enumerate(HALVES):
        for number, offset in enumerate(offsets):
            pltpu.make_async_copy(
                hidden_hbm.at[plane_rows(offset)], ref.hidden.at[half, pl.ds(number * TOK, TOK)], local.at[2]
            ).start()

    routes_here.wait()
    gates_here.wait()
    ref.gates_out[...] = signed_gates(ref.routes[...], ref.gates[...], ref.spread)
    index = iota((PART, 1), 0)
    raw = (((index >> 1) & 7) << 4) + (((low + (index >> 4)) & 7) << 1) + (index & 1)
    ref.order[...] = jnp.where(iota((PART, PART), 1) == raw, 1.0, 0.0).astype(BF16)

    pl.semaphore_wait(barrier, 2 + LOW - 1 + 4)

    for half, offsets in enumerate(HALVES):
        for number, offset in enumerate(offsets):
            remote(
                hidden_hbm.at[plane_rows(offset)],
                ref.hidden_in.at[half, pl.ds(number * TOK, TOK)],
                ref.hidden_sem.at[0, half],
                ref.hidden_sem.at[1, half],
                partner,
            ).start()
    swap_copy = remote(
        queries_hbm.at[pl.ds(QROWS, QROWS)], ref.query_swap, ref.swap_sem.at[0], ref.swap_sem.at[1], sibling
    )

    @pl.when(role == 1)
    def _():
        swap_copy.start()

    def pass_gates(stage):
        for side, step in enumerate((2, -2)):
            source = ref.gates_out
            if stage > 0:
                source = ref.gates_in.at[stage - 1, side]
                wait_for(source, ref.gate_sem.at[1, stage - 1, side])
            if stage < 3:
                remote(
                    source,
                    ref.gates_in.at[stage, side],
                    ref.gate_sem.at[0, stage, side],
                    ref.gate_sem.at[1, stage, side],
                    along_z(step),
                ).start()

    pass_gates(0)

    own_units = pl.ds(pl.multiple_of(tp * HALF, HALF), HALF)
    other_units = pl.ds(pl.multiple_of((1 - tp) * HALF, HALF), HALF)
    wait_for(ref.hidden, local.at[2])
    down_here.wait()
    for half in range(2):
        ref.first_half[half] = dot(ref.hidden[half], ref.down[own_units, :])

    x_sem = ref.x_sem
    for c, chunk in enumerate(CHUNKS):
        half, columns, sent = chunk.half, chunk.columns, chunk.sent * TOK
        if columns.start == 0:
            wait_for(ref.hidden_in.at[half], ref.hidden_sem.at[1, half])
        rows = ref.first_half[half, :, columns] + dot(ref.hidden_in[half], ref.down[other_units, columns])
        rows = rows.astype(BF16)
        ref.first_out[half, 0:sent, columns] = rows[:sent]
        ref.first_in[half, sent:, columns] = rows[sent:]
        for first, blocks, step in chunk.first_hops:
            place = (half, pl.ds(first * TOK, blocks * TOK), columns)
            remote(ref.first_out.at[place], ref.first_in.at[place], x_sem.at[0, c], x_sem.at[1, c], along_z(step)).start()

    pass_gates(1)

    cache_here.wait()
    cache_copy = remote(ref.cache, ref.cache_in, ref.tp_sem.at[2], ref.tp_sem.at[3], partner)
    cache_copy.start()
    queries_here.wait()
    span_here.wait()
    latents = [ref.latents[group].astype(F32) for group in range(2)]
    ref.span[...] = jnp.concatenate(latents + [jnp.zeros((SPAN - 4, LAT), F32)], axis=0).astype(BF16)
    lengths_here.wait()
    destinations_here.wait()
    length = ref.lengths[role * 128 + ep]
    flipped = jnp.broadcast_to(ref.destinations[ep], (QROWS, 1)) != ep
    ask_copy = remote(ref.query_out, ref.query_in, ref.role_sem.at[0], ref.role_sem.at[1], other_role)

    @pl.when(role == 1)
    def _():
        swap_copy.wait_recv()
        swapped = ref.query_swap[...].astype(F32)
        ref.query_out[...] = jnp.where(flipped, swapped, ref.queries[QROWS:, :].astype(F32)).astype(BF16)
        ask_copy.start()

    pass_gates(2)

    def exchange(c):
        chunk = CHUNKS[c]
        half, columns = chunk.half, chunk.columns
        wait_for(ref.first_in.at[half, pl.ds(0, chunk.sent * TOK), columns], x_sem.at[1, c])
        rows = dot(ref.order[...], ref.first_in[half, :, columns]).astype(BF16)
        ref.x_in[half, 0:TOK, columns] = rows[0:TOK]
        ref.x_out[half, :, columns] = rows[TOK:]

        @pl.loop(1, LOW)
        def _(step):
            rows_out = pl.ds(pl.multiple_of(step * TOK - TOK, TOK), TOK)
            rows_in = pl.ds(pl.multiple_of(step * TOK, TOK), TOK)
            remote(
                ref.x_out.at[half, rows_out, columns],
                ref.x_in.at[half, rows_in, columns],
                x_sem.at[2, c],
                x_sem.at[3, c],
                in_plane(step),
            ).start()

    def gate_matrix(c):
        chunk = CHUNKS[c]
        sources = [ref.gates_in[2 if chunk.half == 0 else 0, side] for side in range(2)]
        if chunk.half == 0:
            sources.append(ref.gates_out[...])
        gates = jnp.concatenate(sources, axis=0)
        column = iota((128, PART), 1)
        plane = z + choose((iota((1, PART), 1) >> 1) & 7, chunk.planes)
        mine = iota((128, PART), 0) == (((plane & 15) << 3) + ((low - (column >> 4)) & 7))
        pick_first = jnp.where(mine & ((column & 1) == 0), 1.0, 0.0).astype(BF16)
        pick_second = jnp.where(mine & ((column & 1) == 1), 1.0, 0.0).astype(BF16)
        team = choose((iota((1, PART), 1) >> 1) & 7, chunk.teams)
        same_team = (iota((gates.shape[0], PART), 0) >> 4) == team
        first_high, first_low = split(jnp.maximum(gates, 0.0))
        second_high, second_low = split(jnp.maximum(-gates, 0.0))
        gates_high = jnp.where(same_team, dot(first_high, pick_first) + dot(second_high, pick_second), 0.0)
        gates_low = jnp.where(same_team, dot(first_low, pick_first) + dot(second_low, pick_second), 0.0)
        ref.gates_high[c, 0 : gates.shape[0], :] = gates_high.astype(BF16)
        ref.gates_low[c, 0 : gates.shape[0], :] = gates_low.astype(BF16)

    def combine(c):
        chunk = CHUNKS[c]
        half, columns = chunk.half, chunk.columns
        teams = 48 if half == 0 else 32
        wait_for(ref.x_in.at[half, pl.ds(TOK, PART - TOK), columns], x_sem.at[3, c])
        rows = ref.x_in[half, :, columns]
        sums = dot(ref.gates_high[c, 0:teams, :], rows) + dot(ref.gates_low[c, 0:teams, :], rows)
        ref.second_out[half, :, columns] = sums[:32].astype(BF16)
        if half == 0:
            ref.kept[:, columns] = sums[32:]
        for number, step in enumerate(chunk.second_hops):
            place = (half, pl.ds(number * TOK, TOK), columns)
            remote(ref.second_out.at[place], ref.second_in.at[place], x_sem.at[4, c], x_sem.at[5, c], along_z(step)).start()

    def finish():
        for c, chunk in enumerate(CHUNKS):
            wait_for(ref.second_in.at[chunk.half, :, chunk.columns], x_sem.at[5, c])
        total = ref.kept[...]
        for half in range(2):
            got = ref.second_in[half].astype(F32)
            total = total + (got[0:16] + got[16:32])
        moe_ref[...] = total.astype(BF16)

    keys = (ref.cache, ref.cache_in)
    step_of = iota((QROWS, SPAN), 0) >> 6
    key_of = iota((QROWS, SPAN), 1)
    answer_copy = remote(ref.answer_out, ref.answer_in, ref.role_sem.at[2], ref.role_sem.at[3], other_role)
    back_copy = remote(ref.answer_in, ref.answer_swap, ref.swap_sem.at[2], ref.swap_sem.at[3], sibling)

    def attend_first():
        cache_copy.wait_recv()

        @pl.when(role == 0)
        def _():
            ask_copy.wait_recv()
            top, total, value = scores_of(ref.query_in[...], keys, ref.span, length, tp, key_of < 4)
            ref.answer_out[:, :VLAT] = value.astype(BF16)
            lane = iota((QROWS, 128), 1)
            packed = jnp.zeros((QROWS, 128), F32)
            for number, figure in enumerate((top, total)):
                rest = figure
                for piece in range(3):
                    part = rest.astype(BF16).astype(F32)
                    rest = rest - part
                    packed = jnp.where(lane == number * 3 + piece, part, packed)
            ref.answer_out[:, VLAT:] = packed.astype(BF16)
            answer_copy.start()

    def attend_own():
        _, total, value = scores_of(ref.queries[:QROWS, :], keys, ref.span, length, tp, key_of <= step_of)
        attention_ref[:QROWS, :] = (value / total).astype(BF16)

        @pl.when(role == 0)
        def _():
            _, total, value = scores_of(ref.queries[QROWS:, :], keys, ref.span, length, tp, key_of <= step_of + 2)
            attention_ref[QROWS:, :] = (value / total).astype(BF16)

    def attend_back():
        @pl.when(role == 1)
        def _():
            answer_copy.wait_recv()
            back_copy.start()

    def attend_last():
        @pl.when(role == 1)
        def _():
            own_ok = (key_of >= 2) & (key_of <= step_of + 2)
            top, total, value = scores_of(ref.queries[QROWS:, :], (), ref.span, length, tp, own_ok)
            back_copy.wait_recv()
            answer = jnp.where(flipped, ref.answer_swap[...].astype(F32), ref.answer_in[...].astype(F32))
            figures = answer[:, VLAT:]
            far_top = figures[:, 0:1] + figures[:, 1:2] + figures[:, 2:3]
            far_total = figures[:, 3:4] + figures[:, 4:5] + figures[:, 5:6]
            best = jnp.maximum(top, far_top)
            near, far = jnp.exp(top - best), jnp.exp(far_top - best)
            value = near * value + far * answer[:, :VLAT]
            attention_ref[QROWS:, :] = (value / (near * total + far * far_total)).astype(BF16)

    exchange(0)
    exchange(1)
    pass_gates(3)
    for c in range(3):
        gate_matrix(c)
    exchange(2)
    combine(0)
    combine(1)
    combine(2)
    attend_first()
    attend_own()
    attend_back()
    attend_last()
    finish()

    cache_copy.wait_send()
    for stage in range(3):
        for side in range(2):
            wait_for(ref.gates_out, ref.gate_sem.at[0, stage, side])
    for half in range(2):
        wait_for(ref.hidden_in.at[half], ref.hidden_sem.at[0, half])
    for c, chunk in enumerate(CHUNKS):
        half, columns = chunk.half, chunk.columns
        wait_for(ref.first_out.at[half, pl.ds(0, chunk.sent * TOK), columns], x_sem.at[0, c])
        wait_for(ref.x_out.at[half, :, columns], x_sem.at[2, c])
        wait_for(ref.second_out.at[half, :, columns], x_sem.at[4, c])

    @pl.when(role == 0)
    def _():
        answer_copy.wait_send()

    @pl.when(role == 1)
    def _():
        swap_copy.wait_send()
        ask_copy.wait_send()
        back_copy.wait_send()


def scratch_table():
    dma = pltpu.SemaphoreType.DMA

    def each(rows, kind=BF16):
        return pltpu.VMEM((2, rows, WIDTH), kind)

    return dict(
        routes=pltpu.VMEM((8, TOK), jnp.int32),
        gates=pltpu.VMEM((8, TOK), F32),
        spread=pltpu.VMEM((128, 128), F32),
        hidden=pltpu.VMEM((2, PART, HALF), BF16),
        hidden_in=pltpu.VMEM((2, PART, HALF), BF16),
        order=pltpu.VMEM((PART, PART), BF16),
        down=pltpu.VMEM((2 * HALF, WIDTH), BF16),
        first_half=each(PART, F32),
        cache=pltpu.VMEM((LAT, SHARD), BF16),
        cache_in=pltpu.VMEM((LAT, SHARD), BF16),
        queries=pltpu.VMEM((2 * QROWS, LAT), BF16),
        query_swap=pltpu.VMEM((QROWS, LAT), BF16),
        query_out=pltpu.VMEM((QROWS, LAT), BF16),
        query_in=pltpu.VMEM((QROWS, LAT), BF16),
        answer_out=pltpu.VMEM((QROWS, VLAT + 128), BF16),
        answer_in=pltpu.VMEM((QROWS, VLAT + 128), BF16),
        answer_swap=pltpu.VMEM((QROWS, VLAT + 128), BF16),
        latents=pltpu.VMEM((2, 2, LAT), BF16),
        span=pltpu.VMEM((SPAN, LAT), BF16),
        lengths=pltpu.SMEM((256,), jnp.int32),
        destinations=pltpu.SMEM((128,), jnp.int32),
        gates_out=pltpu.VMEM((TOK, 128), F32),
        gates_in=pltpu.VMEM((3, 2, TOK, 128), F32),
        gates_high=pltpu.VMEM((3, 48, PART), BF16),
        gates_low=pltpu.VMEM((3, 48, PART), BF16),
        x_out=each(PART - TOK),
        x_in=each(PART),
        first_out=each(96),
        first_in=each(PART),
        kept=pltpu.VMEM((TOK, WIDTH), F32),
        second_out=each(32),
        second_in=each(32),
        local_sem=dma((9,)),
        tp_sem=dma((4,)),
        role_sem=dma((4,)),
        swap_sem=dma((4,)),
        gate_sem=dma((2, 3, 2)),
        x_sem=dma((6, 3)),
        hidden_sem=dma((2, 2)),
    )


def named(refs):
    table = scratch_table()
    refs = jax.tree.unflatten(jax.tree.structure(table), refs)
    return types.SimpleNamespace(**refs)


def local(
    routes,
    gate_weights,
    expert_hidden,
    down_weight,
    queries,
    new_latents,
    lengths,
    destinations,
    latent_cache,
):
    moe, attention = pl.pallas_call(
        kernel,
        out_shape=(
            jax.ShapeDtypeStruct((TOK, WIDTH), BF16),
            jax.ShapeDtypeStruct((2 * QROWS, VLAT), BF16),
        ),
        in_specs=[pl.BlockSpec(memory_space=pl.ANY)] * 9,
        out_specs=(pl.BlockSpec(memory_space=pltpu.VMEM),) * 2,
        scratch_shapes=jax.tree.leaves(scratch_table()),
        compiler_params=pltpu.CompilerParams(collective_id=0, has_side_effects=True, vmem_limit_bytes=63 * 2**20),
    )(
        routes.T,
        gate_weights.T,
        expert_hidden[0],
        down_weight[0],
        queries.reshape(2 * QROWS, LAT),
        new_latents[0],
        lengths,
        destinations,
        jnp.swapaxes(latent_cache[0], 0, 1),
    )
    return moe, attention.reshape(1, 2, 2, QROWS // 2, VLAT)


def solution(mesh):
    placed = (
        P(("role", "ep"), None),
        P(("role", "ep"), None),
        P(("role", "ep"), None, "tp"),
        P("ep", None, "tp"),
        P(("role", "ep"), None, None, "tp", None),
        P(("role", "ep"), None, None, None),
        P(),
        P(),
        P(("role", "ep"), "tp", None),
    )
    return jax.shard_map(
        local,
        mesh=mesh,
        in_specs=placed,
        out_specs=(P(("role", "ep"), "tp"), P(("role", "ep"), None, None, "tp", None)),
        check_vma=False,
    )
```

```python
import functools
import types

import jax
import jax.numpy as jnp
from jax import lax
from jax.experimental import pallas as pl
from jax.experimental.pallas import tpu as pltpu
from jax.sharding import PartitionSpec as P

MESH = pl.DeviceIdType.MESH
F32 = jnp.float32
BF16 = jnp.bfloat16

SCORE_SCALE = 0.07216878364870322
VERY_LOW = -1e30
VLAT = 512
LAT = 576
SHARD = 512
PLANES = 16
LOW = 8
TOK = 16
WIDTH = 1792
HALF = 512
QROWS = 128
SPAN = 16
PART = 128
EDGE = 896

FAR = (5, -7, 7, -5, 8, 6, -6, 0)
NEAR = (1, -3, 3, -1, 4, -4, 2, -2)
HALVES = (FAR, NEAR)


class Chunk:
    def __init__(self, half, column, columns):
        self.half = half
        self.kind = 2 if half == 1 else int(column >= EDGE)
        self.columns = pl.ds(column, columns)
        near = half == 1
        left = column < EDGE
        self.sent = 6 if near else 5
        if near:
            far_hops = ((4, 1, -2), (5, 1, 2))
        else:
            far_hops = ((4, 1, -2 if left else 2),)
        self.first_hops = ((0, 2, 1), (2, 2, -1)) + far_hops
        if near:
            self.planes = (-1, -1, 1, 1, 2, -2, 0, 0)
            self.teams = (0, 1, 0, 1, 0, 1, 0, 1)
        else:
            self.planes = (-1, -1, 1, 1, 2 if left else -2, 0, 0, 0)
            self.teams = (0, 1, 0, 1, 0 if left else 1, 0, 1, 2)
        self.second_hops = (-2, 2) if near else (-6, 6)


CHUNKS = tuple(Chunk(*each) for each in ((0, 0, 896), (0, 896, 896), (1, 0, 896), (1, 896, 896)))


def remote(src, dst, send, recv, device):
    return pltpu.make_async_remote_copy(
        src_ref=src, dst_ref=dst, send_sem=send, recv_sem=recv, device_id=device, device_id_type=MESH
    )


def wait_for(ref, sem):
    pltpu.make_async_copy(ref, ref, sem).wait()


def iota(shape, dim):
    return lax.broadcasted_iota(jnp.int32, shape, dim)


def dot(a, b, b_dim=0):
    return lax.dot_general(a, b, (((1,), (b_dim,)), ((), ())), preferred_element_type=F32)


def split(value):
    high = value.astype(BF16)
    return high, (value - high.astype(F32)).astype(BF16)


def choose(index, values):
    result = jnp.zeros_like(index)
    for number, value in enumerate(values):
        result = jnp.where(index == number, value, result)
    return result


def signed_gates(routes, gates, spread):
    names = iota((128, TOK), 0)
    picked = jnp.zeros((128, TOK), F32)
    weight = jnp.zeros((128, TOK), F32)
    for pick in range(routes.shape[0]):
        here = routes[pick : pick + 1, :] == names
        picked = jnp.where(here, 1.0, picked)
        weight = jnp.where(here, gates[pick : pick + 1, :], weight)
    earlier = jnp.where(iota((TOK, TOK), 0) < iota((TOK, TOK), 1), 1.0, 0.0).astype(BF16)
    slot = dot(picked.astype(BF16), earlier)
    spread[...] = jnp.zeros_like(spread)
    spread[:, :TOK] = jnp.where(slot > 0.5, -weight, weight)
    return spread[...].T[:TOK, :]


def scores_of(query, keys, span, length, tp, extra_ok):
    visible = []
    scores = []
    for number, key in enumerate(keys):
        first = (tp if number == 0 else 1 - tp) * SHARD
        ok = iota((1, SHARD), 1) + first < length
        visible.append(ok)
        scores.append(jnp.where(ok, dot(query, key[...]) * SCORE_SCALE, VERY_LOW))
    scores.append(jnp.where(extra_ok, dot(query, span[...], 1) * SCORE_SCALE, VERY_LOW))
    visible.append(extra_ok)
    top = functools.reduce(jnp.maximum, [jnp.max(s, axis=1, keepdims=True) for s in scores])
    parts = [jnp.where(ok, jnp.exp(s - top), 0.0) for s, ok in zip(scores, visible)]
    total = sum(jnp.sum(part, axis=1, keepdims=True) for part in parts)
    value = dot(parts[-1].astype(BF16), span[:, :VLAT])
    for part, key in zip(parts, keys):
        value = value + dot(part.astype(BF16), key[:VLAT, :], 1)
    return top, total, value


def kernel(
    routes_hbm,
    gates_hbm,
    hidden_hbm,
    down_hbm,
    queries_hbm,
    span_hbm,
    lengths_hbm,
    destinations_hbm,
    cache_hbm,
    moe_ref,
    attention_ref,
    *scratch,
):
    ref = named(scratch)

    role, ep, tp = lax.axis_index("role"), lax.axis_index("ep"), lax.axis_index("tp")
    z, low = ep // LOW, ep % LOW

    def along_z(step):
        return {"ep": lax.rem(z + step + PLANES, PLANES) * LOW + low}

    def in_plane(step):
        return {"ep": z * LOW + lax.rem(low + step, LOW)}

    partner = {"tp": 1 - tp}
    other_role = {"role": 1 - role}
    sibling = {"ep": z * LOW + low + 1 - 2 * (low % 2)}

    barrier = pltpu.get_barrier_semaphore()

    def greet(device):
        pl.semaphore_signal(barrier, inc=1, device_id=device, device_id_type=MESH)

    greet(partner)
    greet(other_role)

    @pl.loop(1, LOW)
    def _(step):
        greet(in_plane(step))

    for step in (1, -1, 2, -2):
        greet(along_z(step))

    local = ref.local_sem

    def fetch(number, source, target):
        copy = pltpu.make_async_copy(source, target, local.at[number])
        copy.start()
        return copy

    routes_here = fetch(0, routes_hbm, ref.routes)
    gates_here = fetch(1, gates_hbm, ref.gates)
    down_here = fetch(3, down_hbm, ref.down)
    cache_here = fetch(4, cache_hbm, ref.cache)
    queries_here = fetch(5, queries_hbm, ref.queries)
    span_here = fetch(6, span_hbm, ref.latents)
    lengths_here = fetch(7, lengths_hbm, ref.lengths)
    destinations_here = fetch(8, destinations_hbm, ref.destinations)

    def plane_rows(offset):
        return pl.ds(pl.multiple_of(((z - offset) & 15) * TOK, TOK), TOK)

    for half, offsets in enumerate(HALVES):
        for number, offset in enumerate(offsets):
            pltpu.make_async_copy(
                hidden_hbm.at[plane_rows(offset)], ref.hidden.at[half, pl.ds(number * TOK, TOK)], local.at[2]
            ).start()

    routes_here.wait()
    gates_here.wait()
    ref.gates_out[...] = signed_gates(ref.routes[...], ref.gates[...], ref.spread)
    index = iota((PART, 1), 0)
    raw = (((index >> 1) & 7) << 4) + (((low + (index >> 4)) & 7) << 1) + (index & 1)
    ref.order[...] = jnp.where(iota((PART, PART), 1) == raw, 1.0, 0.0).astype(BF16)

    pl.semaphore_wait(barrier, 2 + LOW - 1 + 4)

    for half, offsets in enumerate(HALVES):
        for number, offset in enumerate(offsets):
            remote(
                hidden_hbm.at[plane_rows(offset)],
                ref.hidden_in.at[half, pl.ds(number * TOK, TOK)],
                ref.hidden_sem.at[0, half],
                ref.hidden_sem.at[1, half],
                partner,
            ).start()
    swap_copy = remote(
        queries_hbm.at[pl.ds(QROWS, QROWS)], ref.query_swap, ref.swap_sem.at[0], ref.swap_sem.at[1], sibling
    )

    @pl.when(role == 1)
    def _():
        swap_copy.start()

    def pass_gates(stage):
        for side, step in enumerate((2, -2)):
            source = ref.gates_out
            if stage > 0:
                source = ref.gates_in.at[stage - 1, side]
                wait_for(source, ref.gate_sem.at[1, stage - 1, side])
            if stage < 3:
                remote(
                    source,
                    ref.gates_in.at[stage, side],
                    ref.gate_sem.at[0, stage, side],
                    ref.gate_sem.at[1, stage, side],
                    along_z(step),
                ).start()

    pass_gates(0)

    own_units = pl.ds(pl.multiple_of(tp * HALF, HALF), HALF)
    other_units = pl.ds(pl.multiple_of((1 - tp) * HALF, HALF), HALF)
    wait_for(ref.hidden, local.at[2])
    down_here.wait()
    for half in range(2):
        ref.first_half[half] = dot(ref.hidden[half], ref.down[own_units, :])
    pass_gates(1)

    x_sem = ref.x_sem
    for c, chunk in enumerate(CHUNKS):
        half, columns, sent = chunk.half, chunk.columns, chunk.sent * TOK
        if columns.start == 0:
            if half == 1:
                pass_gates(2)
            wait_for(ref.hidden_in.at[half], ref.hidden_sem.at[1, half])
        rows = ref.first_half[half, :, columns] + dot(ref.hidden_in[half], ref.down[other_units, columns])
        rows = rows.astype(BF16)
        ref.first_out[half, 0:sent, columns] = rows[:sent]
        ref.first_in[half, sent:, columns] = rows[sent:]
        for first, blocks, step in chunk.first_hops:
            place = (half, pl.ds(first * TOK, blocks * TOK), columns)
            remote(ref.first_out.at[place], ref.first_in.at[place], x_sem.at[0, c], x_sem.at[1, c], along_z(step)).start()

    cache_here.wait()
    cache_copy = remote(ref.cache, ref.cache_in, ref.tp_sem.at[2], ref.tp_sem.at[3], partner)
    cache_copy.start()
    queries_here.wait()
    span_here.wait()
    latents = [ref.latents[group].astype(F32) for group in range(2)]
    ref.span[...] = jnp.concatenate(latents + [jnp.zeros((SPAN - 4, LAT), F32)], axis=0).astype(BF16)
    lengths_here.wait()
    destinations_here.wait()
    length = ref.lengths[role * 128 + ep]
    flipped = jnp.broadcast_to(ref.destinations[ep], (QROWS, 1)) != ep
    ask_copy = remote(ref.query_out, ref.query_in, ref.role_sem.at[0], ref.role_sem.at[1], other_role)

    @pl.when(role == 1)
    def _():
        swap_copy.wait_recv()
        swapped = ref.query_swap[...].astype(F32)
        ref.query_out[...] = jnp.where(flipped, swapped, ref.queries[QROWS:, :].astype(F32)).astype(BF16)
        ask_copy.start()

    def exchange(c):
        chunk = CHUNKS[c]
        half, columns = chunk.half, chunk.columns
        wait_for(ref.first_in.at[half, pl.ds(0, chunk.sent * TOK), columns], x_sem.at[1, c])
        rows = dot(ref.order[...], ref.first_in[half, :, columns]).astype(BF16)
        ref.x_in[half, 0:TOK, columns] = rows[0:TOK]
        ref.x_out[half, :, columns] = rows[TOK:]

        @pl.loop(1, LOW)
        def _(step):
            rows_out = pl.ds(pl.multiple_of(step * TOK - TOK, TOK), TOK)
            rows_in = pl.ds(pl.multiple_of(step * TOK, TOK), TOK)
            remote(
                ref.x_out.at[half, rows_out, columns],
                ref.x_in.at[half, rows_in, columns],
                x_sem.at[2, c],
                x_sem.at[3, c],
                in_plane(step),
            ).start()

    def gate_matrix(chunk):
        sources = [ref.gates_in[2 if chunk.half == 0 else 0, side] for side in range(2)]
        if chunk.half == 0:
            sources.append(ref.gates_out[...])
        gates = jnp.concatenate(sources, axis=0)
        column = iota((128, PART), 1)
        plane = z + choose((iota((1, PART), 1) >> 1) & 7, chunk.planes)
        mine = iota((128, PART), 0) == (((plane & 15) << 3) + ((low - (column >> 4)) & 7))
        pick_first = jnp.where(mine & ((column & 1) == 0), 1.0, 0.0).astype(BF16)
        pick_second = jnp.where(mine & ((column & 1) == 1), 1.0, 0.0).astype(BF16)
        team = choose((iota((1, PART), 1) >> 1) & 7, chunk.teams)
        same_team = (iota((gates.shape[0], PART), 0) >> 4) == team
        first_high, first_low = split(jnp.maximum(gates, 0.0))
        second_high, second_low = split(jnp.maximum(-gates, 0.0))
        gates_high = jnp.where(same_team, dot(first_high, pick_first) + dot(second_high, pick_second), 0.0)
        gates_low = jnp.where(same_team, dot(first_low, pick_first) + dot(second_low, pick_second), 0.0)
        ref.gates_high[chunk.kind, 0 : gates.shape[0], :] = gates_high.astype(BF16)
        ref.gates_low[chunk.kind, 0 : gates.shape[0], :] = gates_low.astype(BF16)

    def combine(c):
        chunk = CHUNKS[c]
        half, columns = chunk.half, chunk.columns
        teams = 48 if half == 0 else 32
        wait_for(ref.x_in.at[half, pl.ds(TOK, PART - TOK), columns], x_sem.at[3, c])
        rows = ref.x_in[half, :, columns]
        sums = dot(ref.gates_high[chunk.kind, 0:teams, :], rows) + dot(ref.gates_low[chunk.kind, 0:teams, :], rows)
        ref.second_out[half, :, columns] = sums[:32].astype(BF16)
        if half == 0:
            ref.kept[:, columns] = sums[32:]
        for number, step in enumerate(chunk.second_hops):
            place = (half, pl.ds(number * TOK, TOK), columns)
            remote(ref.second_out.at[place], ref.second_in.at[place], x_sem.at[4, c], x_sem.at[5, c], along_z(step)).start()

    def finish():
        for c, chunk in enumerate(CHUNKS):
            wait_for(ref.second_in.at[chunk.half, :, chunk.columns], x_sem.at[5, c])
        total = ref.kept[...]
        for half in range(2):
            got = ref.second_in[half].astype(F32)
            total = total + (got[0:16] + got[16:32])
        moe_ref[...] = total.astype(BF16)

    keys = (ref.cache, ref.cache_in)
    step_of = iota((QROWS, SPAN), 0) >> 6
    key_of = iota((QROWS, SPAN), 1)
    answer_copy = remote(ref.answer_out, ref.answer_in, ref.role_sem.at[2], ref.role_sem.at[3], other_role)
    back_copy = remote(ref.answer_in, ref.answer_swap, ref.swap_sem.at[2], ref.swap_sem.at[3], sibling)

    def attend_first():
        cache_copy.wait_recv()

        @pl.when(role == 0)
        def _():
            ask_copy.wait_recv()
            top, total, value = scores_of(ref.query_in[...], keys, ref.span, length, tp, key_of < 4)
            ref.answer_out[:, :VLAT] = value.astype(BF16)
            lane = iota((QROWS, 128), 1)
            packed = jnp.zeros((QROWS, 128), F32)
            for number, figure in enumerate((top, total)):
                rest = figure
                for piece in range(3):
                    part = rest.astype(BF16).astype(F32)
                    rest = rest - part
                    packed = jnp.where(lane == number * 3 + piece, part, packed)
            ref.answer_out[:, VLAT:] = packed.astype(BF16)
            answer_copy.start()

    def attend_own():
        _, total, value = scores_of(ref.queries[:QROWS, :], keys, ref.span, length, tp, key_of <= step_of)
        attention_ref[:QROWS, :] = (value / total).astype(BF16)

        @pl.when(role == 0)
        def _():
            _, total, value = scores_of(ref.queries[QROWS:, :], keys, ref.span, length, tp, key_of <= step_of + 2)
            attention_ref[QROWS:, :] = (value / total).astype(BF16)

    def attend_back():
        @pl.when(role == 1)
        def _():
            answer_copy.wait_recv()
            back_copy.start()

    def attend_last():
        @pl.when(role == 1)
        def _():
            own_ok = (key_of >= 2) & (key_of <= step_of + 2)
            top, total, value = scores_of(ref.queries[QROWS:, :], (), ref.span, length, tp, own_ok)
            back_copy.wait_recv()
            answer = jnp.where(flipped, ref.answer_swap[...].astype(F32), ref.answer_in[...].astype(F32))
            figures = answer[:, VLAT:]
            far_top = figures[:, 0:1] + figures[:, 1:2] + figures[:, 2:3]
            far_total = figures[:, 3:4] + figures[:, 4:5] + figures[:, 5:6]
            best = jnp.maximum(top, far_top)
            near, far = jnp.exp(top - best), jnp.exp(far_top - best)
            value = near * value + far * answer[:, :VLAT]
            attention_ref[QROWS:, :] = (value / (near * total + far * far_total)).astype(BF16)

    exchange(0)
    exchange(1)
    pass_gates(3)
    for chunk in {chunk.kind: chunk for chunk in CHUNKS}.values():
        gate_matrix(chunk)
    exchange(2)
    combine(0)
    exchange(3)
    combine(1)
    combine(2)
    combine(3)
    attend_first()
    attend_own()
    attend_back()
    attend_last()
    finish()

    cache_copy.wait_send()
    for stage in range(3):
        for side in range(2):
            wait_for(ref.gates_out, ref.gate_sem.at[0, stage, side])
    for half in range(2):
        wait_for(ref.hidden_in.at[half], ref.hidden_sem.at[0, half])
    for c, chunk in enumerate(CHUNKS):
        half, columns = chunk.half, chunk.columns
        wait_for(ref.first_out.at[half, pl.ds(0, chunk.sent * TOK), columns], x_sem.at[0, c])
        wait_for(ref.x_out.at[half, :, columns], x_sem.at[2, c])
        wait_for(ref.second_out.at[half, :, columns], x_sem.at[4, c])

    @pl.when(role == 0)
    def _():
        answer_copy.wait_send()

    @pl.when(role == 1)
    def _():
        swap_copy.wait_send()
        ask_copy.wait_send()
        back_copy.wait_send()


def scratch_table():
    dma = pltpu.SemaphoreType.DMA

    def each(rows, kind=BF16):
        return pltpu.VMEM((2, rows, WIDTH), kind)

    return dict(
        routes=pltpu.VMEM((8, TOK), jnp.int32),
        gates=pltpu.VMEM((8, TOK), F32),
        spread=pltpu.VMEM((128, 128), F32),
        hidden=pltpu.VMEM((2, PART, HALF), BF16),
        hidden_in=pltpu.VMEM((2, PART, HALF), BF16),
        order=pltpu.VMEM((PART, PART), BF16),
        down=pltpu.VMEM((2 * HALF, WIDTH), BF16),
        first_half=each(PART, F32),
        cache=pltpu.VMEM((LAT, SHARD), BF16),
        cache_in=pltpu.VMEM((LAT, SHARD), BF16),
        queries=pltpu.VMEM((2 * QROWS, LAT), BF16),
        query_swap=pltpu.VMEM((QROWS, LAT), BF16),
        query_out=pltpu.VMEM((QROWS, LAT), BF16),
        query_in=pltpu.VMEM((QROWS, LAT), BF16),
        answer_out=pltpu.VMEM((QROWS, VLAT + 128), BF16),
        answer_in=pltpu.VMEM((QROWS, VLAT + 128), BF16),
        answer_swap=pltpu.VMEM((QROWS, VLAT + 128), BF16),
        latents=pltpu.VMEM((2, 2, LAT), BF16),
        span=pltpu.VMEM((SPAN, LAT), BF16),
        lengths=pltpu.SMEM((256,), jnp.int32),
        destinations=pltpu.SMEM((128,), jnp.int32),
        gates_out=pltpu.VMEM((TOK, 128), F32),
        gates_in=pltpu.VMEM((3, 2, TOK, 128), F32),
        gates_high=pltpu.VMEM((3, 48, PART), BF16),
        gates_low=pltpu.VMEM((3, 48, PART), BF16),
        x_out=each(PART - TOK),
        x_in=each(PART),
        first_out=each(96),
        first_in=each(PART),
        kept=pltpu.VMEM((TOK, WIDTH), F32),
        second_out=each(32),
        second_in=each(32),
        local_sem=dma((9,)),
        tp_sem=dma((4,)),
        role_sem=dma((4,)),
        swap_sem=dma((4,)),
        gate_sem=dma((2, 3, 2)),
        x_sem=dma((6, len(CHUNKS))),
        hidden_sem=dma((2, 2)),
    )


def named(refs):
    table = scratch_table()
    refs = jax.tree.unflatten(jax.tree.structure(table), refs)
    return types.SimpleNamespace(**refs)


def local(
    routes,
    gate_weights,
    expert_hidden,
    down_weight,
    queries,
    new_latents,
    lengths,
    destinations,
    latent_cache,
):
    operands = (
        routes.T,
        gate_weights.T,
        expert_hidden[0],
        down_weight[0],
        queries.reshape(2 * QROWS, LAT),
        new_latents[0],
        lengths,
        destinations,
        jnp.swapaxes(latent_cache[0], 0, 1),
    )
    operands = [pltpu.with_memory_space_constraint(operand, pltpu.HBM) for operand in operands]
    moe, attention = pl.pallas_call(
        kernel,
        out_shape=(
            jax.ShapeDtypeStruct((TOK, WIDTH), BF16),
            jax.ShapeDtypeStruct((2 * QROWS, VLAT), BF16),
        ),
        in_specs=[pl.BlockSpec(memory_space=pl.ANY)] * 9,
        out_specs=(pl.BlockSpec(memory_space=pltpu.VMEM),) * 2,
        scratch_shapes=jax.tree.leaves(scratch_table()),
        compiler_params=pltpu.CompilerParams(collective_id=0, has_side_effects=True, vmem_limit_bytes=40 * 2**20),
    )(*operands)
    return moe, attention.reshape(1, 2, 2, QROWS // 2, VLAT)


def solution(mesh):
    placed = (
        P(("role", "ep"), None),
        P(("role", "ep"), None),
        P(("role", "ep"), None, "tp"),
        P("ep", None, "tp"),
        P(("role", "ep"), None, None, "tp", None),
        P(("role", "ep"), None, None, None),
        P(),
        P(),
        P(("role", "ep"), "tp", None),
    )
    return jax.shard_map(
        local,
        mesh=mesh,
        in_specs=placed,
        out_specs=(P(("role", "ep"), "tp"), P(("role", "ep"), None, None, "tp", None)),
        check_vma=False,
    )
```

```python
import functools
import types

import jax
import jax.numpy as jnp
from jax import lax
from jax.experimental import pallas as pl
from jax.experimental.pallas import tpu as pltpu
from jax.sharding import PartitionSpec as P

MESH = pl.DeviceIdType.MESH
F32 = jnp.float32
BF16 = jnp.bfloat16

SCORE_SCALE = 0.07216878364870322
VERY_LOW = -1e30
VLAT = 512
LAT = 576
SHARD = 512
PLANES = 16
LOW = 8
TOK = 16
WIDTH = 1792
HALF = 512
QROWS = 128
SPAN = 16
PART = 128
EDGE = 896

FAR = (5, -7, 7, -5, 8, 6, -6, 0)
NEAR = (1, -3, 3, -1, 4, -4, 2, -2)
HALVES = (FAR, NEAR)
PARTS = ((0, 0, 5), (1, 0, 6), (0, 5, 8), (1, 6, 8))


class Chunk:
    def __init__(self, half, column, columns):
        self.half = half
        self.kind = 2 if half == 1 else int(column >= EDGE)
        self.columns = pl.ds(column, columns)
        near = half == 1
        left = column < EDGE
        self.sent = 6 if near else 5
        if near:
            far_hops = ((4, 1, -2), (5, 1, 2))
        else:
            far_hops = ((4, 1, -2 if left else 2),)
        self.first_hops = ((0, 2, 1), (2, 2, -1)) + far_hops
        if near:
            self.planes = (-1, -1, 1, 1, 2, -2, 0, 0)
            self.teams = (0, 1, 0, 1, 0, 1, 0, 1)
        else:
            self.planes = (-1, -1, 1, 1, 2 if left else -2, 0, 0, 0)
            self.teams = (0, 1, 0, 1, 0 if left else 1, 0, 1, 2)
        self.second_hops = (-2, 2) if near else (-6, 6)


CHUNKS = tuple(Chunk(*each) for each in ((0, 0, 896), (0, 896, 896), (1, 0, 1152), (1, 1152, 640)))


def remote(src, dst, send, recv, device):
    return pltpu.make_async_remote_copy(
        src_ref=src, dst_ref=dst, send_sem=send, recv_sem=recv, device_id=device, device_id_type=MESH
    )


def wait_for(ref, sem):
    pltpu.make_async_copy(ref, ref, sem).wait()


def iota(shape, dim):
    return lax.broadcasted_iota(jnp.int32, shape, dim)


def dot(a, b, b_dim=0):
    return lax.dot_general(a, b, (((1,), (b_dim,)), ((), ())), preferred_element_type=F32)


def split(value):
    high = value.astype(BF16)
    return high, (value - high.astype(F32)).astype(BF16)


def choose(index, values):
    result = jnp.zeros_like(index)
    for number, value in enumerate(values):
        result = jnp.where(index == number, value, result)
    return result


def signed_gates(routes, gates, spread):
    names = iota((128, TOK), 0)
    picked = jnp.zeros((128, TOK), F32)
    weight = jnp.zeros((128, TOK), F32)
    for pick in range(routes.shape[0]):
        here = routes[pick : pick + 1, :] == names
        picked = jnp.where(here, 1.0, picked)
        weight = jnp.where(here, gates[pick : pick + 1, :], weight)
    earlier = jnp.where(iota((TOK, TOK), 0) < iota((TOK, TOK), 1), 1.0, 0.0).astype(BF16)
    slot = dot(picked.astype(BF16), earlier)
    spread[...] = jnp.zeros_like(spread)
    spread[:, :TOK] = jnp.where(slot > 0.5, -weight, weight)
    return spread[...].T[:TOK, :]


def scores_of(query, keys, span, length, tp, extra_ok):
    visible = []
    scores = []
    for number, key in enumerate(keys):
        first = (tp if number == 0 else 1 - tp) * SHARD
        ok = iota((1, SHARD), 1) + first < length
        visible.append(ok)
        scores.append(jnp.where(ok, dot(query, key[...]) * SCORE_SCALE, VERY_LOW))
    scores.append(jnp.where(extra_ok, dot(query, span[...], 1) * SCORE_SCALE, VERY_LOW))
    visible.append(extra_ok)
    top = functools.reduce(jnp.maximum, [jnp.max(s, axis=1, keepdims=True) for s in scores])
    parts = [jnp.where(ok, jnp.exp(s - top), 0.0) for s, ok in zip(scores, visible)]
    total = sum(jnp.sum(part, axis=1, keepdims=True) for part in parts)
    value = dot(parts[-1].astype(BF16), span[:, :VLAT])
    for part, key in zip(parts, keys):
        value = value + dot(part.astype(BF16), key[:VLAT, :], 1)
    return top, total, value


def kernel(
    routes_hbm,
    gates_hbm,
    hidden_hbm,
    down_hbm,
    queries_hbm,
    span_hbm,
    lengths_hbm,
    destinations_hbm,
    cache_hbm,
    moe_ref,
    attention_ref,
    *scratch,
):
    ref = named(scratch)

    role, ep, tp = lax.axis_index("role"), lax.axis_index("ep"), lax.axis_index("tp")
    z, low = ep // LOW, ep % LOW

    def along_z(step):
        return {"ep": lax.rem(z + step + PLANES, PLANES) * LOW + low}

    def in_plane(step):
        return {"ep": z * LOW + lax.rem(low + step, LOW)}

    partner = {"tp": 1 - tp}
    other_role = {"role": 1 - role}
    sibling = {"ep": z * LOW + low + 1 - 2 * (low % 2)}

    barrier = pltpu.get_barrier_semaphore()

    def greet(device):
        pl.semaphore_signal(barrier, inc=1, device_id=device, device_id_type=MESH)

    greet(partner)
    greet(other_role)

    @pl.loop(1, LOW)
    def _(step):
        greet(in_plane(step))

    for step in (1, -1, 2, -2):
        greet(along_z(step))

    local = ref.local_sem

    def fetch(number, source, target):
        copy = pltpu.make_async_copy(source, target, local.at[number])
        copy.start()
        return copy

    routes_here = fetch(0, routes_hbm, ref.routes)
    gates_here = fetch(1, gates_hbm, ref.gates)
    down_here = fetch(3, down_hbm, ref.down)
    cache_here = fetch(4, cache_hbm, ref.cache)
    queries_here = fetch(5, queries_hbm, ref.queries)
    span_here = fetch(6, span_hbm, ref.latents)
    lengths_here = fetch(7, lengths_hbm, ref.lengths)
    destinations_here = fetch(8, destinations_hbm, ref.destinations)

    def plane_rows(offset):
        return pl.ds(pl.multiple_of(((z - offset) & 15) * TOK, TOK), TOK)

    for half, offsets in enumerate(HALVES):
        for number, offset in enumerate(offsets):
            pltpu.make_async_copy(
                hidden_hbm.at[plane_rows(offset)], ref.hidden.at[half, pl.ds(number * TOK, TOK)], local.at[2]
            ).start()

    routes_here.wait()
    gates_here.wait()
    ref.gates_out[...] = signed_gates(ref.routes[...], ref.gates[...], ref.spread)
    index = iota((PART, 1), 0)
    raw = (((index >> 1) & 7) << 4) + (((low + (index >> 4)) & 7) << 1) + (index & 1)
    ref.order[...] = jnp.where(iota((PART, PART), 1) == raw, 1.0, 0.0).astype(BF16)

    pl.semaphore_wait(barrier, 2 + LOW - 1 + 4)

    wait_for(ref.hidden, local.at[2])
    for part, (half, first, last) in enumerate(PARTS):
        place = (half, pl.ds(first * TOK, (last - first) * TOK))
        remote(
            ref.hidden.at[place], ref.hidden_in.at[place], ref.hidden_sem.at[0, part], ref.hidden_sem.at[1, part], partner
        ).start()
    swap_copy = remote(
        queries_hbm.at[pl.ds(QROWS, QROWS)], ref.query_swap, ref.swap_sem.at[0], ref.swap_sem.at[1], sibling
    )

    @pl.when(role == 1)
    def _():
        swap_copy.start()

    def pass_gates(stage):
        for side, step in enumerate((2, -2)):
            source = ref.gates_out
            if stage > 0:
                source = ref.gates_in.at[stage - 1, side]
                wait_for(source, ref.gate_sem.at[1, stage - 1, side])
            if stage < 3:
                remote(
                    source,
                    ref.gates_in.at[stage, side],
                    ref.gate_sem.at[0, stage, side],
                    ref.gate_sem.at[1, stage, side],
                    along_z(step),
                ).start()

    pass_gates(0)

    own_units = pl.ds(pl.multiple_of(tp * HALF, HALF), HALF)
    other_units = pl.ds(pl.multiple_of((1 - tp) * HALF, HALF), HALF)
    down_here.wait()
    for half in range(2):
        ref.first_half[half] = dot(ref.hidden[half], ref.down[own_units, :])
    pass_gates(1)

    cache_copy = remote(ref.cache, ref.cache_in, ref.tp_sem.at[2], ref.tp_sem.at[3], partner)

    def send_cache(section):
        @pl.when(role == section)
        def _():
            cache_copy.start()

    cache_here.wait()
    x_sem = ref.x_sem
    for part, (half, first, last) in enumerate(PARTS):
        place = pl.ds(first * TOK, (last - first) * TOK)
        if part == 1:
            pass_gates(2)
        wait_for(ref.hidden_in.at[half, place], ref.hidden_sem.at[1, part])
        if part == 3:
            send_cache(0)
        for c, chunk in enumerate(CHUNKS):
            if chunk.half != half:
                continue
            columns = chunk.columns
            rows = ref.first_half[half, place, columns] + dot(ref.hidden_in[half, place, :], ref.down[other_units, columns])
            if part >= 2:
                ref.first_in[half, place, columns] = rows.astype(BF16)
                continue
            ref.first_out[half, place, columns] = rows.astype(BF16)
            for block, blocks, step in chunk.first_hops:
                sent = (half, pl.ds(block * TOK, blocks * TOK), columns)
                remote(ref.first_out.at[sent], ref.first_in.at[sent], x_sem.at[0, c], x_sem.at[1, c], along_z(step)).start()

    queries_here.wait()
    span_here.wait()
    latents = [ref.latents[group].astype(F32) for group in range(2)]
    ref.span[...] = jnp.concatenate(latents + [jnp.zeros((SPAN - 4, LAT), F32)], axis=0).astype(BF16)
    lengths_here.wait()
    destinations_here.wait()
    length = ref.lengths[role * 128 + ep]
    flipped = jnp.broadcast_to(ref.destinations[ep], (QROWS, 1)) != ep
    ask_copy = remote(ref.query_out, ref.query_in, ref.role_sem.at[0], ref.role_sem.at[1], other_role)

    @pl.when(role == 1)
    def _():
        swap_copy.wait_recv()
        swapped = ref.query_swap[...].astype(F32)
        ref.query_out[...] = jnp.where(flipped, swapped, ref.queries[QROWS:, :].astype(F32)).astype(BF16)
        ask_copy.start()

    def exchange(c):
        chunk = CHUNKS[c]
        half, columns = chunk.half, chunk.columns
        wait_for(ref.first_in.at[half, pl.ds(0, chunk.sent * TOK), columns], x_sem.at[1, c])
        rows = dot(ref.order[...], ref.first_in[half, :, columns]).astype(BF16)
        ref.x_in[half, 0:TOK, columns] = rows[0:TOK]
        ref.x_out[half, :, columns] = rows[TOK:]

        @pl.loop(1, LOW)
        def _(step):
            rows_out = pl.ds(pl.multiple_of(step * TOK - TOK, TOK), TOK)
            rows_in = pl.ds(pl.multiple_of(step * TOK, TOK), TOK)
            remote(
                ref.x_out.at[half, rows_out, columns],
                ref.x_in.at[half, rows_in, columns],
                x_sem.at[2, c],
                x_sem.at[3, c],
                in_plane(step),
            ).start()

    def gate_matrix(chunk):
        sources = [ref.gates_in[2 if chunk.half == 0 else 0, side] for side in range(2)]
        if chunk.half == 0:
            sources.append(ref.gates_out[...])
        gates = jnp.concatenate(sources, axis=0)
        column = iota((128, PART), 1)
        plane = z + choose((iota((1, PART), 1) >> 1) & 7, chunk.planes)
        mine = iota((128, PART), 0) == (((plane & 15) << 3) + ((low - (column >> 4)) & 7))
        pick_first = jnp.where(mine & ((column & 1) == 0), 1.0, 0.0).astype(BF16)
        pick_second = jnp.where(mine & ((column & 1) == 1), 1.0, 0.0).astype(BF16)
        team = choose((iota((1, PART), 1) >> 1) & 7, chunk.teams)
        same_team = (iota((gates.shape[0], PART), 0) >> 4) == team
        first_high, first_low = split(jnp.maximum(gates, 0.0))
        second_high, second_low = split(jnp.maximum(-gates, 0.0))
        gates_high = jnp.where(same_team, dot(first_high, pick_first) + dot(second_high, pick_second), 0.0)
        gates_low = jnp.where(same_team, dot(first_low, pick_first) + dot(second_low, pick_second), 0.0)
        ref.gates_high[chunk.kind, 0 : gates.shape[0], :] = gates_high.astype(BF16)
        ref.gates_low[chunk.kind, 0 : gates.shape[0], :] = gates_low.astype(BF16)

    def combine(c):
        chunk = CHUNKS[c]
        half, columns = chunk.half, chunk.columns
        teams = 48 if half == 0 else 32
        wait_for(ref.x_in.at[half, pl.ds(TOK, PART - TOK), columns], x_sem.at[3, c])
        rows = ref.x_in[half, :, columns]
        sums = dot(ref.gates_high[chunk.kind, 0:teams, :], rows) + dot(ref.gates_low[chunk.kind, 0:teams, :], rows)
        ref.second_out[half, :, columns] = sums[:32].astype(BF16)
        if half == 0:
            ref.kept[:, columns] = sums[32:]
        for number, step in enumerate(chunk.second_hops):
            place = (half, pl.ds(number * TOK, TOK), columns)
            remote(ref.second_out.at[place], ref.second_in.at[place], x_sem.at[4, c], x_sem.at[5, c], along_z(step)).start()

    def finish():
        for c, chunk in enumerate(CHUNKS):
            wait_for(ref.second_in.at[chunk.half, :, chunk.columns], x_sem.at[5, c])
        total = ref.kept[...]
        for half in range(2):
            got = ref.second_in[half].astype(F32)
            total = total + (got[0:16] + got[16:32])
        moe_ref[...] = total.astype(BF16)

    keys = (ref.cache, ref.cache_in)
    step_of = iota((QROWS, SPAN), 0) >> 6
    key_of = iota((QROWS, SPAN), 1)
    answer_copy = remote(ref.answer_out, ref.answer_in, ref.role_sem.at[2], ref.role_sem.at[3], other_role)
    back_copy = remote(ref.answer_in, ref.answer_swap, ref.swap_sem.at[2], ref.swap_sem.at[3], sibling)

    def attend_first():
        cache_copy.wait_recv()

        @pl.when(role == 0)
        def _():
            ask_copy.wait_recv()
            top, total, value = scores_of(ref.query_in[...], keys, ref.span, length, tp, key_of < 4)
            ref.answer_out[:, :VLAT] = value.astype(BF16)
            lane = iota((QROWS, 128), 1)
            packed = jnp.zeros((QROWS, 128), F32)
            for number, figure in enumerate((top, total)):
                rest = figure
                for piece in range(3):
                    part = rest.astype(BF16).astype(F32)
                    rest = rest - part
                    packed = jnp.where(lane == number * 3 + piece, part, packed)
            ref.answer_out[:, VLAT:] = packed.astype(BF16)
            answer_copy.start()

    def attend_own():
        _, total, value = scores_of(ref.queries[:QROWS, :], keys, ref.span, length, tp, key_of <= step_of)
        attention_ref[:QROWS, :] = (value / total).astype(BF16)

        @pl.when(role == 0)
        def _():
            _, total, value = scores_of(ref.queries[QROWS:, :], keys, ref.span, length, tp, key_of <= step_of + 2)
            attention_ref[QROWS:, :] = (value / total).astype(BF16)

    def attend_back():
        @pl.when(role == 1)
        def _():
            answer_copy.wait_recv()
            back_copy.start()

    def attend_last():
        @pl.when(role == 1)
        def _():
            own_ok = (key_of >= 2) & (key_of <= step_of + 2)
            top, total, value = scores_of(ref.queries[QROWS:, :], (), ref.span, length, tp, own_ok)
            back_copy.wait_recv()
            answer = jnp.where(flipped, ref.answer_swap[...].astype(F32), ref.answer_in[...].astype(F32))
            figures = answer[:, VLAT:]
            far_top = figures[:, 0:1] + figures[:, 1:2] + figures[:, 2:3]
            far_total = figures[:, 3:4] + figures[:, 4:5] + figures[:, 5:6]
            best = jnp.maximum(top, far_top)
            near, far = jnp.exp(top - best), jnp.exp(far_top - best)
            value = near * value + far * answer[:, :VLAT]
            attention_ref[QROWS:, :] = (value / (near * total + far * far_total)).astype(BF16)

    exchange(0)
    exchange(1)
    send_cache(1)
    pass_gates(3)
    for chunk in {chunk.kind: chunk for chunk in CHUNKS}.values():
        gate_matrix(chunk)
    exchange(2)
    combine(0)
    exchange(3)
    combine(1)
    combine(2)
    combine(3)
    attend_first()
    attend_own()
    attend_back()
    attend_last()
    finish()

    cache_copy.wait_send()
    for stage in range(3):
        for side in range(2):
            wait_for(ref.gates_out, ref.gate_sem.at[0, stage, side])
    for part, (half, first, last) in enumerate(PARTS):
        wait_for(ref.hidden_in.at[half, pl.ds(first * TOK, (last - first) * TOK)], ref.hidden_sem.at[0, part])
    for c, chunk in enumerate(CHUNKS):
        half, columns = chunk.half, chunk.columns
        wait_for(ref.first_out.at[half, pl.ds(0, chunk.sent * TOK), columns], x_sem.at[0, c])
        wait_for(ref.x_out.at[half, :, columns], x_sem.at[2, c])
        wait_for(ref.second_out.at[half, :, columns], x_sem.at[4, c])

    @pl.when(role == 0)
    def _():
        answer_copy.wait_send()

    @pl.when(role == 1)
    def _():
        swap_copy.wait_send()
        ask_copy.wait_send()
        back_copy.wait_send()


def scratch_table():
    dma = pltpu.SemaphoreType.DMA

    def each(rows, kind=BF16):
        return pltpu.VMEM((2, rows, WIDTH), kind)

    return dict(
        routes=pltpu.VMEM((8, TOK), jnp.int32),
        gates=pltpu.VMEM((8, TOK), F32),
        spread=pltpu.VMEM((128, 128), F32),
        hidden=pltpu.VMEM((2, PART, HALF), BF16),
        hidden_in=pltpu.VMEM((2, PART, HALF), BF16),
        order=pltpu.VMEM((PART, PART), BF16),
        down=pltpu.VMEM((2 * HALF, WIDTH), BF16),
        first_half=each(PART, F32),
        cache=pltpu.VMEM((LAT, SHARD), BF16),
        cache_in=pltpu.VMEM((LAT, SHARD), BF16),
        queries=pltpu.VMEM((2 * QROWS, LAT), BF16),
        query_swap=pltpu.VMEM((QROWS, LAT), BF16),
        query_out=pltpu.VMEM((QROWS, LAT), BF16),
        query_in=pltpu.VMEM((QROWS, LAT), BF16),
        answer_out=pltpu.VMEM((QROWS, VLAT + 128), BF16),
        answer_in=pltpu.VMEM((QROWS, VLAT + 128), BF16),
        answer_swap=pltpu.VMEM((QROWS, VLAT + 128), BF16),
        latents=pltpu.VMEM((2, 2, LAT), BF16),
        span=pltpu.VMEM((SPAN, LAT), BF16),
        lengths=pltpu.SMEM((256,), jnp.int32),
        destinations=pltpu.SMEM((128,), jnp.int32),
        gates_out=pltpu.VMEM((TOK, 128), F32),
        gates_in=pltpu.VMEM((3, 2, TOK, 128), F32),
        gates_high=pltpu.VMEM((3, 48, PART), BF16),
        gates_low=pltpu.VMEM((3, 48, PART), BF16),
        x_out=each(PART - TOK),
        x_in=each(PART),
        first_out=each(96),
        first_in=each(PART),
        kept=pltpu.VMEM((TOK, WIDTH), F32),
        second_out=each(32),
        second_in=each(32),
        local_sem=dma((9,)),
        tp_sem=dma((4,)),
        role_sem=dma((4,)),
        swap_sem=dma((4,)),
        gate_sem=dma((2, 3, 2)),
        x_sem=dma((6, len(CHUNKS))),
        hidden_sem=dma((2, 4)),
    )


def named(refs):
    table = scratch_table()
    refs = jax.tree.unflatten(jax.tree.structure(table), refs)
    return types.SimpleNamespace(**refs)


def local(
    routes,
    gate_weights,
    expert_hidden,
    down_weight,
    queries,
    new_latents,
    lengths,
    destinations,
    latent_cache,
):
    operands = (
        routes.T,
        gate_weights.T,
        expert_hidden[0],
        down_weight[0],
        queries.reshape(2 * QROWS, LAT),
        new_latents[0],
        lengths,
        destinations,
        jnp.swapaxes(latent_cache[0], 0, 1),
    )
    operands = [pltpu.with_memory_space_constraint(operand, pltpu.HBM) for operand in operands]
    moe, attention = pl.pallas_call(
        kernel,
        out_shape=(
            jax.ShapeDtypeStruct((TOK, WIDTH), BF16),
            jax.ShapeDtypeStruct((2 * QROWS, VLAT), BF16),
        ),
        in_specs=[pl.BlockSpec(memory_space=pl.ANY)] * 9,
        out_specs=(pl.BlockSpec(memory_space=pltpu.VMEM),) * 2,
        scratch_shapes=jax.tree.leaves(scratch_table()),
        compiler_params=pltpu.CompilerParams(collective_id=0, has_side_effects=True, vmem_limit_bytes=40 * 2**20),
    )(*operands)
    return moe, attention.reshape(1, 2, 2, QROWS // 2, VLAT)


def solution(mesh):
    placed = (
        P(("role", "ep"), None),
        P(("role", "ep"), None),
        P(("role", "ep"), None, "tp"),
        P("ep", None, "tp"),
        P(("role", "ep"), None, None, "tp", None),
        P(("role", "ep"), None, None, None),
        P(),
        P(),
        P(("role", "ep"), "tp", None),
    )
    return jax.shard_map(
        local,
        mesh=mesh,
        in_specs=placed,
        out_specs=(P(("role", "ep"), "tp"), P(("role", "ep"), None, None, "tp", None)),
        check_vma=False,
    )
```

```python
import functools
import types

import jax
import jax.numpy as jnp
from jax import lax
from jax.experimental import pallas as pl
from jax.experimental.pallas import tpu as pltpu
from jax.sharding import PartitionSpec as P

MESH = pl.DeviceIdType.MESH
F32 = jnp.float32
BF16 = jnp.bfloat16

SCORE_SCALE = 0.07216878364870322
VERY_LOW = -1e30
VLAT = 512
LAT = 576
SHARD = 512
PLANES = 16
LOW = 8
TOK = 16
WIDTH = 1792
HALF = 512
QROWS = 128
SPAN = 16
PART = 128
EDGE = 896

FAR = (5, -7, 7, -5, 8, 6, -6, 0)
NEAR = (1, -3, 3, -1, 4, -4, 2, -2)
HALVES = (FAR, NEAR)
PARTS = ((0, 0, 5), (1, 0, 6), (0, 5, 8), (1, 6, 8))


class Chunk:
    def __init__(self, half, column, columns):
        self.half = half
        self.kind = 2 if half == 1 else int(column >= EDGE)
        self.columns = pl.ds(column, columns)
        near = half == 1
        left = column < EDGE
        self.sent = 6 if near else 5
        if near:
            far_hops = ((4, 1, -2), (5, 1, 2))
        else:
            far_hops = ((4, 1, -2 if left else 2),)
        self.first_hops = ((0, 2, 1), (2, 2, -1)) + far_hops
        if near:
            self.planes = (-1, -1, 1, 1, 2, -2, 0, 0)
            self.teams = (0, 1, 0, 1, 0, 1, 0, 1)
        else:
            self.planes = (-1, -1, 1, 1, 2 if left else -2, 0, 0, 0)
            self.teams = (0, 1, 0, 1, 0 if left else 1, 0, 1, 2)
        self.second_hops = (-2, 2) if near else (-6, 6)


CHUNKS = tuple(Chunk(*each) for each in ((0, 0, 896), (0, 896, 896), (1, 0, 1152), (1, 1152, 640)))


def remote(src, dst, send, recv, device):
    return pltpu.make_async_remote_copy(
        src_ref=src, dst_ref=dst, send_sem=send, recv_sem=recv, device_id=device, device_id_type=MESH
    )


def wait_for(ref, sem):
    pltpu.make_async_copy(ref, ref, sem).wait()


def iota(shape, dim):
    return lax.broadcasted_iota(jnp.int32, shape, dim)


def dot(a, b, b_dim=0):
    return lax.dot_general(a, b, (((1,), (b_dim,)), ((), ())), preferred_element_type=F32)


def split(value):
    high = value.astype(BF16)
    return high, (value - high.astype(F32)).astype(BF16)


def choose(index, values):
    result = jnp.zeros_like(index)
    for number, value in enumerate(values):
        result = jnp.where(index == number, value, result)
    return result


def signed_gates(routes, gates, spread):
    names = iota((128, TOK), 0)
    picked = jnp.zeros((128, TOK), F32)
    weight = jnp.zeros((128, TOK), F32)
    for pick in range(routes.shape[0]):
        here = routes[pick : pick + 1, :] == names
        picked = jnp.where(here, 1.0, picked)
        weight = jnp.where(here, gates[pick : pick + 1, :], weight)
    earlier = jnp.where(iota((TOK, TOK), 0) < iota((TOK, TOK), 1), 1.0, 0.0).astype(BF16)
    slot = dot(picked.astype(BF16), earlier)
    spread[...] = jnp.zeros_like(spread)
    spread[:, :TOK] = jnp.where(slot > 0.5, -weight, weight)
    return spread[...].T[:TOK, :]


def scores_of(query, keys, span, length, tp, extra_ok):
    visible = []
    scores = []
    for number, key in enumerate(keys):
        first = (tp if number == 0 else 1 - tp) * SHARD
        ok = iota((1, SHARD), 1) + first < length
        visible.append(ok)
        scores.append(jnp.where(ok, dot(query, key[...]) * SCORE_SCALE, VERY_LOW))
    scores.append(jnp.where(extra_ok, dot(query, span[...], 1) * SCORE_SCALE, VERY_LOW))
    visible.append(extra_ok)
    top = functools.reduce(jnp.maximum, [jnp.max(s, axis=1, keepdims=True) for s in scores])
    parts = [jnp.where(ok, jnp.exp(s - top), 0.0) for s, ok in zip(scores, visible)]
    total = sum(jnp.sum(part, axis=1, keepdims=True) for part in parts)
    value = dot(parts[-1].astype(BF16), span[:, :VLAT])
    for part, key in zip(parts, keys):
        value = value + dot(part.astype(BF16), key[:VLAT, :], 1)
    return top, total, value


def kernel(
    routes_hbm,
    gates_hbm,
    hidden_hbm,
    down_hbm,
    queries_hbm,
    span_hbm,
    lengths_hbm,
    destinations_hbm,
    cache_hbm,
    moe_ref,
    attention_ref,
    *scratch,
):
    ref = named(scratch)

    role, ep, tp = lax.axis_index("role"), lax.axis_index("ep"), lax.axis_index("tp")
    z, low = ep // LOW, ep % LOW

    def along_z(step):
        return {"ep": lax.rem(z + step + PLANES, PLANES) * LOW + low}

    def in_plane(step):
        return {"ep": z * LOW + lax.rem(low + step, LOW)}

    partner = {"tp": 1 - tp}
    other_role = {"role": 1 - role}
    sibling = {"ep": z * LOW + low + 1 - 2 * (low % 2)}

    barrier = pltpu.get_barrier_semaphore()

    def greet(device):
        pl.semaphore_signal(barrier, inc=1, device_id=device, device_id_type=MESH)

    greet(partner)
    greet(other_role)

    @pl.loop(1, LOW)
    def _(step):
        greet(in_plane(step))

    for step in (1, -1, 2, -2):
        greet(along_z(step))

    local = ref.local_sem

    def fetch(number, source, target):
        copy = pltpu.make_async_copy(source, target, local.at[number])
        copy.start()
        return copy

    routes_here = fetch(0, routes_hbm, ref.routes)
    gates_here = fetch(1, gates_hbm, ref.gates)
    down_here = fetch(3, down_hbm, ref.down)
    cache_here = fetch(4, cache_hbm, ref.cache)
    queries_here = fetch(5, queries_hbm, ref.queries)
    span_here = fetch(6, span_hbm, ref.latents)
    lengths_here = fetch(7, lengths_hbm, ref.lengths)
    destinations_here = fetch(8, destinations_hbm, ref.destinations)

    def plane_rows(offset):
        return pl.ds(pl.multiple_of(((z - offset) & 15) * TOK, TOK), TOK)

    for half, offsets in enumerate(HALVES):
        for number, offset in enumerate(offsets):
            pltpu.make_async_copy(
                hidden_hbm.at[plane_rows(offset)], ref.hidden.at[half, pl.ds(number * TOK, TOK)], local.at[2]
            ).start()

    routes_here.wait()
    gates_here.wait()
    ref.gates_out[...] = signed_gates(ref.routes[...], ref.gates[...], ref.spread)
    index = iota((PART, 1), 0)
    raw = (((index >> 1) & 7) << 4) + (((low + (index >> 4)) & 7) << 1) + (index & 1)
    ref.order[...] = jnp.where(iota((PART, PART), 1) == raw, 1.0, 0.0).astype(BF16)

    pl.semaphore_wait(barrier, 2 + LOW - 1 + 4)

    wait_for(ref.hidden, local.at[2])
    for part, (half, first, last) in enumerate(PARTS):
        place = (half, pl.ds(first * TOK, (last - first) * TOK))
        remote(
            ref.hidden.at[place], ref.hidden_in.at[place], ref.hidden_sem.at[0, part], ref.hidden_sem.at[1, part], partner
        ).start()
    swap_copy = remote(
        queries_hbm.at[pl.ds(QROWS, QROWS)], ref.query_swap, ref.swap_sem.at[0], ref.swap_sem.at[1], sibling
    )

    @pl.when(role == 1)
    def _():
        swap_copy.start()

    def pass_gates(stage):
        for side, step in enumerate((2, -2)):
            source = ref.gates_out
            if stage > 0:
                source = ref.gates_in.at[stage - 1, side]
                wait_for(source, ref.gate_sem.at[1, stage - 1, side])
            if stage < 3:
                remote(
                    source,
                    ref.gates_in.at[stage, side],
                    ref.gate_sem.at[0, stage, side],
                    ref.gate_sem.at[1, stage, side],
                    along_z(step),
                ).start()

    pass_gates(0)

    own_units = pl.ds(pl.multiple_of(tp * HALF, HALF), HALF)
    other_units = pl.ds(pl.multiple_of((1 - tp) * HALF, HALF), HALF)
    down_here.wait()
    for half in range(2):
        ref.first_half[half] = dot(ref.hidden[half], ref.down[own_units, :])
    pass_gates(1)

    cache_copy = remote(ref.cache, ref.cache_in, ref.tp_sem.at[2], ref.tp_sem.at[3], partner)

    def send_cache(section):
        @pl.when(role == section)
        def _():
            cache_copy.start()

    cache_here.wait()
    x_sem = ref.x_sem
    for part, (half, first, last) in enumerate(PARTS):
        place = pl.ds(first * TOK, (last - first) * TOK)
        if part == 1:
            pass_gates(2)
        wait_for(ref.hidden_in.at[half, place], ref.hidden_sem.at[1, part])
        if part == 3:
            send_cache(0)
        for c, chunk in enumerate(CHUNKS):
            if chunk.half != half:
                continue
            columns = chunk.columns
            rows = ref.first_half[half, place, columns] + dot(ref.hidden_in[half, place, :], ref.down[other_units, columns])
            if part >= 2:
                ref.first_in[half, place, columns] = rows.astype(BF16)
                continue
            ref.first_out[half, place, columns] = rows.astype(BF16)
            for block, blocks, step in chunk.first_hops:
                sent = (half, pl.ds(block * TOK, blocks * TOK), columns)
                remote(ref.first_out.at[sent], ref.first_in.at[sent], x_sem.at[0, c], x_sem.at[1, c], along_z(step)).start()

    queries_here.wait()
    span_here.wait()
    latents = [ref.latents[group].astype(F32) for group in range(2)]
    ref.span[...] = jnp.concatenate(latents + [jnp.zeros((SPAN - 4, LAT), F32)], axis=0).astype(BF16)
    lengths_here.wait()
    destinations_here.wait()
    length = ref.lengths[role * 128 + ep]
    flipped = jnp.broadcast_to(ref.destinations[ep], (QROWS, 1)) != ep
    ask_copy = remote(ref.query_out, ref.query_in, ref.role_sem.at[0], ref.role_sem.at[1], other_role)

    @pl.when(role == 1)
    def _():
        swap_copy.wait_recv()
        swapped = ref.query_swap[...].astype(F32)
        ref.query_out[...] = jnp.where(flipped, swapped, ref.queries[QROWS:, :].astype(F32)).astype(BF16)
        ask_copy.start()

    def exchange(c):
        chunk = CHUNKS[c]
        half, columns = chunk.half, chunk.columns
        wait_for(ref.first_in.at[half, pl.ds(0, chunk.sent * TOK), columns], x_sem.at[1, c])
        rows = dot(ref.order[...], ref.first_in[half, :, columns]).astype(BF16)
        ref.x_in[half, 0:TOK, columns] = rows[0:TOK]
        ref.x_out[half, :, columns] = rows[TOK:]

        @pl.loop(1, LOW)
        def _(step):
            step = LOW - step
            rows_out = pl.ds(pl.multiple_of(step * TOK - TOK, TOK), TOK)
            rows_in = pl.ds(pl.multiple_of(step * TOK, TOK), TOK)
            remote(
                ref.x_out.at[half, rows_out, columns],
                ref.x_in.at[half, rows_in, columns],
                x_sem.at[2, c],
                x_sem.at[3, c],
                in_plane(step),
            ).start()

    def gate_matrix(chunk):
        sources = [ref.gates_in[2 if chunk.half == 0 else 0, side] for side in range(2)]
        if chunk.half == 0:
            sources.append(ref.gates_out[...])
        gates = jnp.concatenate(sources, axis=0)
        column = iota((128, PART), 1)
        plane = z + choose((iota((1, PART), 1) >> 1) & 7, chunk.planes)
        mine = iota((128, PART), 0) == (((plane & 15) << 3) + ((low - (column >> 4)) & 7))
        pick_first = jnp.where(mine & ((column & 1) == 0), 1.0, 0.0).astype(BF16)
        pick_second = jnp.where(mine & ((column & 1) == 1), 1.0, 0.0).astype(BF16)
        team = choose((iota((1, PART), 1) >> 1) & 7, chunk.teams)
        same_team = (iota((gates.shape[0], PART), 0) >> 4) == team
        first_high, first_low = split(jnp.maximum(gates, 0.0))
        second_high, second_low = split(jnp.maximum(-gates, 0.0))
        gates_high = jnp.where(same_team, dot(first_high, pick_first) + dot(second_high, pick_second), 0.0)
        gates_low = jnp.where(same_team, dot(first_low, pick_first) + dot(second_low, pick_second), 0.0)
        ref.gates_high[chunk.kind, 0 : gates.shape[0], :] = gates_high.astype(BF16)
        ref.gates_low[chunk.kind, 0 : gates.shape[0], :] = gates_low.astype(BF16)

    def combine(c):
        chunk = CHUNKS[c]
        half, columns = chunk.half, chunk.columns
        teams = 48 if half == 0 else 32
        wait_for(ref.x_in.at[half, pl.ds(TOK, PART - TOK), columns], x_sem.at[3, c])
        rows = ref.x_in[half, :, columns]
        sums = dot(ref.gates_high[chunk.kind, 0:teams, :], rows) + dot(ref.gates_low[chunk.kind, 0:teams, :], rows)
        ref.second_out[half, :, columns] = sums[:32].astype(BF16)
        if half == 0:
            ref.kept[:, columns] = sums[32:]
        for number, step in enumerate(chunk.second_hops):
            place = (half, pl.ds(number * TOK, TOK), columns)
            remote(ref.second_out.at[place], ref.second_in.at[place], x_sem.at[4, c], x_sem.at[5, c], along_z(step)).start()

    def finish():
        for c, chunk in enumerate(CHUNKS):
            wait_for(ref.second_in.at[chunk.half, :, chunk.columns], x_sem.at[5, c])
        total = ref.kept[...]
        for half in range(2):
            got = ref.second_in[half].astype(F32)
            total = total + (got[0:16] + got[16:32])
        moe_ref[...] = total.astype(BF16)

    keys = (ref.cache, ref.cache_in)
    step_of = iota((QROWS, SPAN), 0) >> 6
    key_of = iota((QROWS, SPAN), 1)
    answer_copy = remote(ref.answer_out, ref.answer_in, ref.role_sem.at[2], ref.role_sem.at[3], other_role)
    back_copy = remote(ref.answer_in, ref.answer_swap, ref.swap_sem.at[2], ref.swap_sem.at[3], sibling)

    def attend_first():
        @pl.when(role == 0)
        def _():
            cache_copy.wait_recv()
            ask_copy.wait_recv()
            top, total, value = scores_of(ref.query_in[...], keys, ref.span, length, tp, key_of < 4)
            ref.answer_out[:, :VLAT] = value.astype(BF16)
            lane = iota((QROWS, 128), 1)
            packed = jnp.zeros((QROWS, 128), F32)
            for number, figure in enumerate((top, total)):
                rest = figure
                for piece in range(3):
                    part = rest.astype(BF16).astype(F32)
                    rest = rest - part
                    packed = jnp.where(lane == number * 3 + piece, part, packed)
            ref.answer_out[:, VLAT:] = packed.astype(BF16)
            answer_copy.start()

    def attend_own():
        @pl.when(role == 1)
        def _():
            cache_copy.wait_recv()

        _, total, value = scores_of(ref.queries[:QROWS, :], keys, ref.span, length, tp, key_of <= step_of)
        attention_ref[:QROWS, :] = (value / total).astype(BF16)

        @pl.when(role == 0)
        def _():
            _, total, value = scores_of(ref.queries[QROWS:, :], keys, ref.span, length, tp, key_of <= step_of + 2)
            attention_ref[QROWS:, :] = (value / total).astype(BF16)

    def attend_back():
        @pl.when(role == 1)
        def _():
            answer_copy.wait_recv()
            back_copy.start()

    def attend_last():
        @pl.when(role == 1)
        def _():
            own_ok = (key_of >= 2) & (key_of <= step_of + 2)
            top, total, value = scores_of(ref.queries[QROWS:, :], (), ref.span, length, tp, own_ok)
            back_copy.wait_recv()
            answer = jnp.where(flipped, ref.answer_swap[...].astype(F32), ref.answer_in[...].astype(F32))
            figures = answer[:, VLAT:]
            far_top = figures[:, 0:1] + figures[:, 1:2] + figures[:, 2:3]
            far_total = figures[:, 3:4] + figures[:, 4:5] + figures[:, 5:6]
            best = jnp.maximum(top, far_top)
            near, far = jnp.exp(top - best), jnp.exp(far_top - best)
            value = near * value + far * answer[:, :VLAT]
            attention_ref[QROWS:, :] = (value / (near * total + far * far_total)).astype(BF16)

    exchange(0)
    exchange(1)
    send_cache(1)
    pass_gates(3)
    for chunk in {chunk.kind: chunk for chunk in CHUNKS}.values():
        gate_matrix(chunk)
    exchange(2)
    combine(0)
    exchange(3)
    combine(1)
    combine(2)
    combine(3)
    attend_first()
    attend_back()
    attend_own()
    attend_last()
    finish()

    cache_copy.wait_send()
    for stage in range(3):
        for side in range(2):
            wait_for(ref.gates_out, ref.gate_sem.at[0, stage, side])
    for part, (half, first, last) in enumerate(PARTS):
        wait_for(ref.hidden_in.at[half, pl.ds(first * TOK, (last - first) * TOK)], ref.hidden_sem.at[0, part])
    for c, chunk in enumerate(CHUNKS):
        half, columns = chunk.half, chunk.columns
        wait_for(ref.first_out.at[half, pl.ds(0, chunk.sent * TOK), columns], x_sem.at[0, c])
        wait_for(ref.x_out.at[half, :, columns], x_sem.at[2, c])
        wait_for(ref.second_out.at[half, :, columns], x_sem.at[4, c])

    @pl.when(role == 0)
    def _():
        answer_copy.wait_send()

    @pl.when(role == 1)
    def _():
        swap_copy.wait_send()
        ask_copy.wait_send()
        back_copy.wait_send()


def scratch_table():
    dma = pltpu.SemaphoreType.DMA

    def each(rows, kind=BF16):
        return pltpu.VMEM((2, rows, WIDTH), kind)

    return dict(
        routes=pltpu.VMEM((8, TOK), jnp.int32),
        gates=pltpu.VMEM((8, TOK), F32),
        spread=pltpu.VMEM((128, 128), F32),
        hidden=pltpu.VMEM((2, PART, HALF), BF16),
        hidden_in=pltpu.VMEM((2, PART, HALF), BF16),
        order=pltpu.VMEM((PART, PART), BF16),
        down=pltpu.VMEM((2 * HALF, WIDTH), BF16),
        first_half=each(PART, F32),
        cache=pltpu.VMEM((LAT, SHARD), BF16),
        cache_in=pltpu.VMEM((LAT, SHARD), BF16),
        queries=pltpu.VMEM((2 * QROWS, LAT), BF16),
        query_swap=pltpu.VMEM((QROWS, LAT), BF16),
        query_out=pltpu.VMEM((QROWS, LAT), BF16),
        query_in=pltpu.VMEM((QROWS, LAT), BF16),
        answer_out=pltpu.VMEM((QROWS, VLAT + 128), BF16),
        answer_in=pltpu.VMEM((QROWS, VLAT + 128), BF16),
        answer_swap=pltpu.VMEM((QROWS, VLAT + 128), BF16),
        latents=pltpu.VMEM((2, 2, LAT), BF16),
        span=pltpu.VMEM((SPAN, LAT), BF16),
        lengths=pltpu.SMEM((256,), jnp.int32),
        destinations=pltpu.SMEM((128,), jnp.int32),
        gates_out=pltpu.VMEM((TOK, 128), F32),
        gates_in=pltpu.VMEM((3, 2, TOK, 128), F32),
        gates_high=pltpu.VMEM((3, 48, PART), BF16),
        gates_low=pltpu.VMEM((3, 48, PART), BF16),
        x_out=each(PART - TOK),
        x_in=each(PART),
        first_out=each(96),
        first_in=each(PART),
        kept=pltpu.VMEM((TOK, WIDTH), F32),
        second_out=each(32),
        second_in=each(32),
        local_sem=dma((9,)),
        tp_sem=dma((4,)),
        role_sem=dma((4,)),
        swap_sem=dma((4,)),
        gate_sem=dma((2, 3, 2)),
        x_sem=dma((6, len(CHUNKS))),
        hidden_sem=dma((2, 4)),
    )


def named(refs):
    table = scratch_table()
    refs = jax.tree.unflatten(jax.tree.structure(table), refs)
    return types.SimpleNamespace(**refs)


def local(
    routes,
    gate_weights,
    expert_hidden,
    down_weight,
    queries,
    new_latents,
    lengths,
    destinations,
    latent_cache,
):
    operands = (
        routes.T,
        gate_weights.T,
        expert_hidden[0],
        down_weight[0],
        queries.reshape(2 * QROWS, LAT),
        new_latents[0],
        lengths,
        destinations,
        jnp.swapaxes(latent_cache[0], 0, 1),
    )
    operands = [pltpu.with_memory_space_constraint(operand, pltpu.HBM) for operand in operands]
    moe, attention = pl.pallas_call(
        kernel,
        out_shape=(
            jax.ShapeDtypeStruct((TOK, WIDTH), BF16),
            jax.ShapeDtypeStruct((2 * QROWS, VLAT), BF16),
        ),
        in_specs=[pl.BlockSpec(memory_space=pl.ANY)] * 9,
        out_specs=(pl.BlockSpec(memory_space=pltpu.VMEM),) * 2,
        scratch_shapes=jax.tree.leaves(scratch_table()),
        compiler_params=pltpu.CompilerParams(collective_id=0, has_side_effects=True, vmem_limit_bytes=40 * 2**20),
    )(*operands)
    return moe, attention.reshape(1, 2, 2, QROWS // 2, VLAT)


def solution(mesh):
    placed = (
        P(("role", "ep"), None),
        P(("role", "ep"), None),
        P(("role", "ep"), None, "tp"),
        P("ep", None, "tp"),
        P(("role", "ep"), None, None, "tp", None),
        P(("role", "ep"), None, None, None),
        P(),
        P(),
        P(("role", "ep"), "tp", None),
    )
    return jax.shard_map(
        local,
        mesh=mesh,
        in_specs=placed,
        out_specs=(P(("role", "ep"), "tp"), P(("role", "ep"), None, None, "tp", None)),
        check_vma=False,
    )
```

```python
import functools
import types

import jax
import jax.numpy as jnp
from jax import lax
from jax.experimental import pallas as pl
from jax.experimental.pallas import tpu as pltpu
from jax.sharding import PartitionSpec as P

MESH = pl.DeviceIdType.MESH
F32 = jnp.float32
BF16 = jnp.bfloat16

SCORE_SCALE = 0.07216878364870322
VERY_LOW = -1e30
VLAT = 512
LAT = 576
SHARD = 512
PLANES = 16
LOW = 8
TOK = 16
WIDTH = 1792
HALF = 512
QROWS = 128
SPAN = 16
PART = 128
EDGE = 896

FAR = (5, -7, 7, -5, 8, 6, -6, 0)
NEAR = (1, -3, 3, -1, 4, -4, 2, -2)
HALVES = (FAR, NEAR)
PARTS = ((0, 0, 5), (1, 0, 6), (0, 5, 8), (1, 6, 8))


class Chunk:
    def __init__(self, half, column, columns):
        self.half = half
        self.kind = 2 if half == 1 else int(column >= EDGE)
        self.columns = pl.ds(column, columns)
        near = half == 1
        left = column < EDGE
        self.sent = 6 if near else 5
        if near:
            far_hops = ((4, 1, -2), (5, 1, 2))
        else:
            far_hops = ((4, 1, -2 if left else 2),)
        self.first_hops = ((0, 2, 1), (2, 2, -1)) + far_hops
        if near:
            self.planes = (-1, -1, 1, 1, 2, -2, 0, 0)
            self.teams = (0, 1, 0, 1, 0, 1, 0, 1)
        else:
            self.planes = (-1, -1, 1, 1, 2 if left else -2, 0, 0, 0)
            self.teams = (0, 1, 0, 1, 0 if left else 1, 0, 1, 2)
        self.second_hops = (-2, 2) if near else (-6, 6)


CHUNKS = tuple(Chunk(*each) for each in ((0, 0, 896), (0, 896, 896), (1, 0, 1152), (1, 1152, 640)))


def remote(src, dst, send, recv, device):
    return pltpu.make_async_remote_copy(
        src_ref=src, dst_ref=dst, send_sem=send, recv_sem=recv, device_id=device, device_id_type=MESH
    )


def wait_for(ref, sem):
    pltpu.make_async_copy(ref, ref, sem).wait()


def iota(shape, dim):
    return lax.broadcasted_iota(jnp.int32, shape, dim)


def dot(a, b, b_dim=0):
    return lax.dot_general(a, b, (((1,), (b_dim,)), ((), ())), preferred_element_type=F32)


def split(value):
    high = value.astype(BF16)
    return high, (value - high.astype(F32)).astype(BF16)


def choose(index, values):
    result = jnp.zeros_like(index)
    for number, value in enumerate(values):
        result = jnp.where(index == number, value, result)
    return result


def signed_gates(routes, gates, spread):
    names = iota((128, TOK), 0)
    picked = jnp.zeros((128, TOK), F32)
    weight = jnp.zeros((128, TOK), F32)
    for pick in range(routes.shape[0]):
        here = routes[pick : pick + 1, :] == names
        picked = jnp.where(here, 1.0, picked)
        weight = jnp.where(here, gates[pick : pick + 1, :], weight)
    earlier = jnp.where(iota((TOK, TOK), 0) < iota((TOK, TOK), 1), 1.0, 0.0).astype(BF16)
    slot = dot(picked.astype(BF16), earlier)
    spread[...] = jnp.zeros_like(spread)
    spread[:, :TOK] = jnp.where(slot > 0.5, -weight, weight)
    return spread[...].T[:TOK, :]


def scores_of(query, keys, span, length, tp, extra_ok):
    visible = []
    scores = []
    for number, key in enumerate(keys):
        first = (tp if number == 0 else 1 - tp) * SHARD
        ok = iota((1, SHARD), 1) + first < length
        visible.append(ok)
        scores.append(jnp.where(ok, dot(query, key[...]) * SCORE_SCALE, VERY_LOW))
    scores.append(jnp.where(extra_ok, dot(query, span[...], 1) * SCORE_SCALE, VERY_LOW))
    visible.append(extra_ok)
    top = functools.reduce(jnp.maximum, [jnp.max(s, axis=1, keepdims=True) for s in scores])
    parts = [jnp.where(ok, jnp.exp(s - top), 0.0) for s, ok in zip(scores, visible)]
    total = sum(jnp.sum(part, axis=1, keepdims=True) for part in parts)
    value = dot(parts[-1].astype(BF16), span[:, :VLAT])
    for part, key in zip(parts, keys):
        value = value + dot(part.astype(BF16), key[:VLAT, :], 1)
    return top, total, value


def kernel(
    routes_hbm,
    gates_hbm,
    hidden_hbm,
    down_hbm,
    queries_hbm,
    span_hbm,
    lengths_hbm,
    destinations_hbm,
    cache_hbm,
    moe_ref,
    attention_ref,
    *scratch,
):
    ref = named(scratch)

    role, ep, tp = lax.axis_index("role"), lax.axis_index("ep"), lax.axis_index("tp")
    z, low = ep // LOW, ep % LOW

    def along_z(step):
        return {"ep": lax.rem(z + step + PLANES, PLANES) * LOW + low}

    def in_plane(step):
        return {"ep": z * LOW + lax.rem(low + step, LOW)}

    partner = {"tp": 1 - tp}
    other_role = {"role": 1 - role}
    sibling = {"ep": z * LOW + low + 1 - 2 * (low % 2)}

    barrier = pltpu.get_barrier_semaphore()

    def greet(device):
        pl.semaphore_signal(barrier, inc=1, device_id=device, device_id_type=MESH)

    greet(partner)
    greet(other_role)

    @pl.loop(1, LOW)
    def _(step):
        greet(in_plane(step))

    for step in (1, -1, 2, -2):
        greet(along_z(step))

    local = ref.local_sem

    def fetch(number, source, target):
        copy = pltpu.make_async_copy(source, target, local.at[number])
        copy.start()
        return copy

    routes_here = fetch(0, routes_hbm, ref.routes)
    gates_here = fetch(1, gates_hbm, ref.gates)
    down_here = fetch(3, down_hbm, ref.down)
    cache_here = fetch(4, cache_hbm, ref.cache)
    queries_here = fetch(5, queries_hbm, ref.queries)
    span_here = fetch(6, span_hbm, ref.span)
    lengths_here = fetch(7, lengths_hbm, ref.lengths)
    destinations_here = fetch(8, destinations_hbm, ref.destinations)

    def plane_rows(offset):
        return pl.ds(pl.multiple_of(((z - offset) & 15) * TOK, TOK), TOK)

    for half, offsets in enumerate(HALVES):
        for number, offset in enumerate(offsets):
            pltpu.make_async_copy(
                hidden_hbm.at[plane_rows(offset)], ref.hidden.at[half, pl.ds(number * TOK, TOK)], local.at[2]
            ).start()

    routes_here.wait()
    gates_here.wait()
    ref.gates_out[...] = signed_gates(ref.routes[...], ref.gates[...], ref.spread)
    index = iota((PART, 1), 0)
    raw = (((index >> 1) & 7) << 4) + (((low + (index >> 4)) & 7) << 1) + (index & 1)
    ref.order[...] = jnp.where(iota((PART, PART), 1) == raw, 1.0, 0.0).astype(BF16)

    pl.semaphore_wait(barrier, 2 + LOW - 1 + 4)

    wait_for(ref.hidden, local.at[2])
    for part, (half, first, last) in enumerate(PARTS):
        place = (half, pl.ds(first * TOK, (last - first) * TOK))
        remote(
            ref.hidden.at[place], ref.hidden_in.at[place], ref.hidden_sem.at[0, part], ref.hidden_sem.at[1, part], partner
        ).start()
    swap_copy = remote(
        queries_hbm.at[pl.ds(QROWS, QROWS)], ref.query_swap, ref.swap_sem.at[0], ref.swap_sem.at[1], sibling
    )

    @pl.when(role == 1)
    def _():
        swap_copy.start()

    def pass_gates(stage):
        for side, step in enumerate((2, -2)):
            source = ref.gates_out
            if stage > 0:
                source = ref.gates_in.at[stage - 1, side]
                wait_for(source, ref.gate_sem.at[1, stage - 1, side])
            if stage < 3:
                remote(
                    source,
                    ref.gates_in.at[stage, side],
                    ref.gate_sem.at[0, stage, side],
                    ref.gate_sem.at[1, stage, side],
                    along_z(step),
                ).start()

    pass_gates(0)

    own_units = pl.ds(pl.multiple_of(tp * HALF, HALF), HALF)
    other_units = pl.ds(pl.multiple_of((1 - tp) * HALF, HALF), HALF)
    down_here.wait()
    for half in range(2):
        ref.first_half[half] = dot(ref.hidden[half], ref.down[own_units, :])
    pass_gates(1)

    cache_copy = remote(ref.cache, ref.cache_in, ref.tp_sem.at[2], ref.tp_sem.at[3], partner)

    def send_cache(section):
        @pl.when(role == section)
        def _():
            cache_copy.start()

    cache_here.wait()
    x_sem = ref.x_sem
    for part, (half, first, last) in enumerate(PARTS):
        place = pl.ds(first * TOK, (last - first) * TOK)
        if part == 1:
            pass_gates(2)
        wait_for(ref.hidden_in.at[half, place], ref.hidden_sem.at[1, part])
        if part == 3:
            send_cache(0)
        for c, chunk in enumerate(CHUNKS):
            if chunk.half != half:
                continue
            columns = chunk.columns
            rows = ref.first_half[half, place, columns] + dot(ref.hidden_in[half, place, :], ref.down[other_units, columns])
            if part >= 2:
                ref.first_in[half, place, columns] = rows.astype(BF16)
                continue
            ref.first_out[half, place, columns] = rows.astype(BF16)
            for block, blocks, step in chunk.first_hops:
                sent = (half, pl.ds(block * TOK, blocks * TOK), columns)
                remote(ref.first_out.at[sent], ref.first_in.at[sent], x_sem.at[0, c], x_sem.at[1, c], along_z(step)).start()

    queries_here.wait()
    span_here.wait()
    lengths_here.wait()
    destinations_here.wait()
    length = ref.lengths[role * 128 + ep]
    flipped = jnp.broadcast_to(ref.destinations[ep], (QROWS, 1)) != ep
    ask_copy = remote(ref.query_out, ref.query_in, ref.role_sem.at[0], ref.role_sem.at[1], other_role)

    @pl.when(role == 1)
    def _():
        swap_copy.wait_recv()
        swapped = ref.query_swap[...].astype(F32)
        ref.query_out[...] = jnp.where(flipped, swapped, ref.queries[QROWS:, :].astype(F32)).astype(BF16)
        ask_copy.start()

    def exchange(c):
        chunk = CHUNKS[c]
        half, columns = chunk.half, chunk.columns
        wait_for(ref.first_in.at[half, pl.ds(0, chunk.sent * TOK), columns], x_sem.at[1, c])
        rows = dot(ref.order[...], ref.first_in[half, :, columns]).astype(BF16)
        ref.x_in[half, 0:TOK, columns] = rows[0:TOK]
        ref.x_out[half, :, columns] = rows[TOK:]

        @pl.loop(1, LOW)
        def _(step):
            step = LOW - step
            rows_out = pl.ds(pl.multiple_of(step * TOK - TOK, TOK), TOK)
            rows_in = pl.ds(pl.multiple_of(step * TOK, TOK), TOK)
            remote(
                ref.x_out.at[half, rows_out, columns],
                ref.x_in.at[half, rows_in, columns],
                x_sem.at[2, c],
                x_sem.at[3, c],
                in_plane(step),
            ).start()

    def gate_matrix(chunk):
        sources = [ref.gates_in[2 if chunk.half == 0 else 0, side] for side in range(2)]
        if chunk.half == 0:
            sources.append(ref.gates_out[...])
        gates = jnp.concatenate(sources, axis=0)
        column = iota((128, PART), 1)
        plane = z + choose((iota((1, PART), 1) >> 1) & 7, chunk.planes)
        mine = iota((128, PART), 0) == (((plane & 15) << 3) + ((low - (column >> 4)) & 7))
        pick_first = jnp.where(mine & ((column & 1) == 0), 1.0, 0.0).astype(BF16)
        pick_second = jnp.where(mine & ((column & 1) == 1), 1.0, 0.0).astype(BF16)
        team = choose((iota((1, PART), 1) >> 1) & 7, chunk.teams)
        same_team = (iota((gates.shape[0], PART), 0) >> 4) == team
        first_high, first_low = split(jnp.maximum(gates, 0.0))
        second_high, second_low = split(jnp.maximum(-gates, 0.0))
        gates_high = jnp.where(same_team, dot(first_high, pick_first) + dot(second_high, pick_second), 0.0)
        gates_low = jnp.where(same_team, dot(first_low, pick_first) + dot(second_low, pick_second), 0.0)
        ref.gates_high[chunk.kind, 0 : gates.shape[0], :] = gates_high.astype(BF16)
        ref.gates_low[chunk.kind, 0 : gates.shape[0], :] = gates_low.astype(BF16)

    def combine(c):
        chunk = CHUNKS[c]
        half, columns = chunk.half, chunk.columns
        teams = 48 if half == 0 else 32
        wait_for(ref.x_in.at[half, pl.ds(TOK, PART - TOK), columns], x_sem.at[3, c])
        rows = ref.x_in[half, :, columns]
        sums = dot(ref.gates_high[chunk.kind, 0:teams, :], rows) + dot(ref.gates_low[chunk.kind, 0:teams, :], rows)
        ref.second_out[half, :, columns] = sums[:32].astype(BF16)
        if half == 0:
            ref.kept[:, columns] = sums[32:]
        for number, step in enumerate(chunk.second_hops):
            place = (half, pl.ds(number * TOK, TOK), columns)
            remote(ref.second_out.at[place], ref.second_in.at[place], x_sem.at[4, c], x_sem.at[5, c], along_z(step)).start()

    def finish():
        for c, chunk in enumerate(CHUNKS):
            wait_for(ref.second_in.at[chunk.half, :, chunk.columns], x_sem.at[5, c])
        total = ref.kept[...]
        for half in range(2):
            got = ref.second_in[half].astype(F32)
            total = total + (got[0:16] + got[16:32])
        moe_ref[...] = total.astype(BF16)

    keys = (ref.cache, ref.cache_in)
    step_of = iota((QROWS, SPAN), 0) >> 6
    key_of = iota((QROWS, SPAN), 1)
    answer_copy = remote(ref.answer_out, ref.answer_in, ref.role_sem.at[2], ref.role_sem.at[3], other_role)
    back_copy = remote(ref.answer_in, ref.answer_swap, ref.swap_sem.at[2], ref.swap_sem.at[3], sibling)

    def attend_first():
        @pl.when(role == 0)
        def _():
            cache_copy.wait_recv()
            ask_copy.wait_recv()
            top, total, value = scores_of(ref.query_in[...], keys, ref.span, length, tp, key_of < 4)
            ref.answer_out[:, :VLAT] = value.astype(BF16)
            lane = iota((QROWS, 128), 1)
            packed = jnp.zeros((QROWS, 128), F32)
            for number, figure in enumerate((top, total)):
                rest = figure
                for piece in range(3):
                    part = rest.astype(BF16).astype(F32)
                    rest = rest - part
                    packed = jnp.where(lane == number * 3 + piece, part, packed)
            ref.answer_out[:, VLAT:] = packed.astype(BF16)
            answer_copy.start()

    def attend_own():
        @pl.when(role == 1)
        def _():
            cache_copy.wait_recv()

        _, total, value = scores_of(ref.queries[:QROWS, :], keys, ref.span, length, tp, key_of <= step_of)
        attention_ref[:QROWS, :] = (value / total).astype(BF16)

        @pl.when(role == 0)
        def _():
            _, total, value = scores_of(ref.queries[QROWS:, :], keys, ref.span, length, tp, key_of <= step_of + 2)
            attention_ref[QROWS:, :] = (value / total).astype(BF16)

    def attend_back():
        @pl.when(role == 1)
        def _():
            answer_copy.wait_recv()
            back_copy.start()

    def attend_last():
        @pl.when(role == 1)
        def _():
            own_ok = (key_of >= 2) & (key_of <= step_of + 2)
            top, total, value = scores_of(ref.queries[QROWS:, :], (), ref.span, length, tp, own_ok)
            back_copy.wait_recv()
            answer = jnp.where(flipped, ref.answer_swap[...].astype(F32), ref.answer_in[...].astype(F32))
            figures = answer[:, VLAT:]
            far_top = figures[:, 0:1] + figures[:, 1:2] + figures[:, 2:3]
            far_total = figures[:, 3:4] + figures[:, 4:5] + figures[:, 5:6]
            best = jnp.maximum(top, far_top)
            near, far = jnp.exp(top - best), jnp.exp(far_top - best)
            value = near * value + far * answer[:, :VLAT]
            attention_ref[QROWS:, :] = (value / (near * total + far * far_total)).astype(BF16)

    exchange(0)
    exchange(1)
    send_cache(1)
    pass_gates(3)
    for chunk in {chunk.kind: chunk for chunk in CHUNKS}.values():
        gate_matrix(chunk)
    exchange(2)
    combine(0)
    exchange(3)
    combine(1)
    combine(2)
    combine(3)
    attend_first()
    attend_back()
    attend_own()
    attend_last()
    finish()

    cache_copy.wait_send()
    for stage in range(3):
        for side in range(2):
            wait_for(ref.gates_out, ref.gate_sem.at[0, stage, side])
    for part, (half, first, last) in enumerate(PARTS):
        wait_for(ref.hidden_in.at[half, pl.ds(first * TOK, (last - first) * TOK)], ref.hidden_sem.at[0, part])
    for c, chunk in enumerate(CHUNKS):
        half, columns = chunk.half, chunk.columns
        wait_for(ref.first_out.at[half, pl.ds(0, chunk.sent * TOK), columns], x_sem.at[0, c])
        wait_for(ref.x_out.at[half, :, columns], x_sem.at[2, c])
        wait_for(ref.second_out.at[half, :, columns], x_sem.at[4, c])

    @pl.when(role == 0)
    def _():
        answer_copy.wait_send()

    @pl.when(role == 1)
    def _():
        swap_copy.wait_send()
        ask_copy.wait_send()
        back_copy.wait_send()


def scratch_table():
    dma = pltpu.SemaphoreType.DMA

    def each(rows, kind=BF16):
        return pltpu.VMEM((2, rows, WIDTH), kind)

    return dict(
        routes=pltpu.VMEM((8, TOK), jnp.int32),
        gates=pltpu.VMEM((8, TOK), F32),
        spread=pltpu.VMEM((128, 128), F32),
        hidden=pltpu.VMEM((2, PART, HALF), BF16),
        hidden_in=pltpu.VMEM((2, PART, HALF), BF16),
        order=pltpu.VMEM((PART, PART), BF16),
        down=pltpu.VMEM((2 * HALF, WIDTH), BF16),
        first_half=each(PART, F32),
        cache=pltpu.VMEM((LAT, SHARD), BF16),
        cache_in=pltpu.VMEM((LAT, SHARD), BF16),
        queries=pltpu.VMEM((2 * QROWS, LAT), BF16),
        query_swap=pltpu.VMEM((QROWS, LAT), BF16),
        query_out=pltpu.VMEM((QROWS, LAT), BF16),
        query_in=pltpu.VMEM((QROWS, LAT), BF16),
        answer_out=pltpu.VMEM((QROWS, VLAT + 128), BF16),
        answer_in=pltpu.VMEM((QROWS, VLAT + 128), BF16),
        answer_swap=pltpu.VMEM((QROWS, VLAT + 128), BF16),
        span=pltpu.VMEM((SPAN, LAT), BF16),
        lengths=pltpu.SMEM((256,), jnp.int32),
        destinations=pltpu.SMEM((128,), jnp.int32),
        gates_out=pltpu.VMEM((TOK, 128), F32),
        gates_in=pltpu.VMEM((3, 2, TOK, 128), F32),
        gates_high=pltpu.VMEM((3, 48, PART), BF16),
        gates_low=pltpu.VMEM((3, 48, PART), BF16),
        x_out=each(PART - TOK),
        x_in=each(PART),
        first_out=each(96),
        first_in=each(PART),
        kept=pltpu.VMEM((TOK, WIDTH), F32),
        second_out=each(32),
        second_in=each(32),
        local_sem=dma((9,)),
        tp_sem=dma((4,)),
        role_sem=dma((4,)),
        swap_sem=dma((4,)),
        gate_sem=dma((2, 3, 2)),
        x_sem=dma((6, len(CHUNKS))),
        hidden_sem=dma((2, 4)),
    )


def named(refs):
    table = scratch_table()
    refs = jax.tree.unflatten(jax.tree.structure(table), refs)
    return types.SimpleNamespace(**refs)


def local(
    routes,
    gate_weights,
    expert_hidden,
    down_weight,
    queries,
    new_latents,
    lengths,
    destinations,
    latent_cache,
):
    operands = (
        routes.T,
        gate_weights.T,
        expert_hidden[0],
        down_weight[0],
        queries.reshape(2 * QROWS, LAT),
        jnp.pad(new_latents.reshape(4, LAT), ((0, SPAN - 4), (0, 0))),
        lengths,
        destinations,
        jnp.swapaxes(latent_cache[0], 0, 1),
    )
    operands = [pltpu.with_memory_space_constraint(operand, pltpu.HBM) for operand in operands]
    moe, attention = pl.pallas_call(
        kernel,
        out_shape=(
            jax.ShapeDtypeStruct((TOK, WIDTH), BF16),
            jax.ShapeDtypeStruct((2 * QROWS, VLAT), BF16),
        ),
        in_specs=[pl.BlockSpec(memory_space=pl.ANY)] * 9,
        out_specs=(pl.BlockSpec(memory_space=pltpu.VMEM),) * 2,
        scratch_shapes=jax.tree.leaves(scratch_table()),
        compiler_params=pltpu.CompilerParams(collective_id=0, has_side_effects=True, vmem_limit_bytes=40 * 2**20),
    )(*operands)
    return moe, attention.reshape(1, 2, 2, QROWS // 2, VLAT)


def solution(mesh):
    placed = (
        P(("role", "ep"), None),
        P(("role", "ep"), None),
        P(("role", "ep"), None, "tp"),
        P("ep", None, "tp"),
        P(("role", "ep"), None, None, "tp", None),
        P(("role", "ep"), None, None, None),
        P(),
        P(),
        P(("role", "ep"), "tp", None),
    )
    return jax.shard_map(
        local,
        mesh=mesh,
        in_specs=placed,
        out_specs=(P(("role", "ep"), "tp"), P(("role", "ep"), None, None, "tp", None)),
        check_vma=False,
    )
```
